256 devices in a mesh: section: 2 (over x_lo), row: 16 (over y, x_hi, core), col: 8 (over z).
Axes of the slice: x: 4 (x_hi: 2, x_lo: 2; x = x_hi * 2 + x_lo), y: 4, z: 8, core: 2. Of those that a mesh axis runs over, the one named last changes fastest.
Arguments:
- fwd_in: bfloat16 [2, 384, 8192], P('section', 'col', 'row'), may hold values from -6 to 6
- bwd_in: bfloat16 [2, 384, 8192], P('section', 'col', 'row'), may hold values from -6 to 6
- cotangent: bfloat16 [2, 384, 8192], P('section', 'col', 'row'), may hold values from -6 to 6
- w_gate: bfloat16 [2, 8192, 14336], P('section', 'row', 'col'), may hold values from -0.0625 to 0.0625
- w_up: bfloat16 [2, 8192, 14336], P('section', 'row', 'col'), may hold values from -0.0625 to 0.0625
- w_down: bfloat16 [2, 14336, 8192], P('section', 'col', 'row'), may hold values from -0.046875 to 0.046875
Outputs:
- next_inputs: bfloat16 [2, 384, 8192], P('section', ('row', 'col'))
- next_grads: bfloat16 [2, 384, 8192], P('section', ('row', 'col'))
- grad_gate: bfloat16 [2, 8192, 14336], P('section', 'row', 'col')
- grad_up: bfloat16 [2, 8192, 14336], P('section', 'row', 'col')
- grad_down: bfloat16 [2, 14336, 8192], P('section', 'col', 'row')
The draws below stay inside these ranges and needn't reach their ends.
All inputs are finite; a program needn't handle non-finite values.
Results may differ from the reference program's by a relative error of at most 0.027.
Values may be sent and summed in bfloat16 or wider, within the bound.
A program may use at most 64 MiB of HBM per device.

```python
import jax
import jax.numpy as jnp
from jax import lax

D = 8192
FF = 14336
TOKENS = 384
SECTIONS = 2
N_ROW = 16


def block_levels(stream_key, extent, split, low, high):
    loudness = 1.0
    for dim, blocks in split:
        draws = jax.random.uniform(jax.random.fold_in(jax.random.fold_in(stream_key, 6), dim), (blocks,), jnp.float32, low / len(split), high / len(split))
        loudness = loudness * jnp.repeat(jnp.exp(draws), extent[dim] // blocks).reshape((-1,) + (1,) * (len(extent) - 1 - dim))
    return loudness


def noise(stream_key, shape, deviation, reach, cuts=(), dtype=jnp.bfloat16):
    level = block_levels(stream_key, shape, cuts, -0.22, 0.18) if cuts else 1.0
    array = jax.random.normal(stream_key, shape, jnp.float32) * deviation * level
    return jnp.minimum(jnp.maximum(array, -reach), reach).astype(dtype)


def setup_inputs(seed: int = 0) -> dict:
    key_list = jax.random.split(jax.random.key(seed), 7)
    return {
        "fwd_in": noise(key_list[0], (SECTIONS, TOKENS, D), 1.0, 6.0, ((0, 2), (1, 8), (2, 16))),
        "bwd_in": noise(key_list[1], (SECTIONS, TOKENS, D), 1.0, 6.0, ((0, 2), (1, 8), (2, 16))),
        "cotangent": noise(key_list[2], (SECTIONS, TOKENS, D), 1.0, 6.0, ((0, 2), (1, 8), (2, 16))),
        "w_gate": noise(key_list[3], (SECTIONS, D, FF), D ** -0.5, 0.0625, ((0, 2), (1, 16), (2, 8))),
        "w_up": noise(key_list[4], (SECTIONS, D, FF), D ** -0.5, 0.0625, ((0, 2), (1, 16), (2, 8))),
        "w_down": noise(key_list[5], (SECTIONS, FF, D), FF ** -0.5, 0.046875, ((0, 2), (1, 8), (2, 16))),
    }


def blocked(left, right, parts):
    inner = left.shape[1] // parts
    total = jnp.zeros((left.shape[0], right.shape[1]), jnp.float32)
    for index in range(parts):
        piece = jnp.dot(left[:, index * inner:(index + 1) * inner], right[index * inner:(index + 1) * inner], preferred_element_type=jnp.float32)
        rounded = lax.optimization_barrier(piece.astype(jnp.bfloat16))
        total = total + rounded.astype(jnp.float32)
    return total


def section_work(fresh, stored, incoming, gate_weight, up_weight, down_weight):
    gate_new = blocked(fresh, gate_weight, N_ROW)
    up_new = blocked(fresh, up_weight, N_ROW)
    gate_old = blocked(stored, gate_weight, N_ROW)
    up_old = blocked(stored, up_weight, N_ROW)
    d_act = blocked(incoming, jnp.transpose(down_weight), N_ROW)
    sig_new = jax.nn.sigmoid(gate_new)
    sig_old = jax.nn.sigmoid(gate_old)
    act_new = (gate_new * sig_new * up_new).astype(jnp.bfloat16)
    act_old = (gate_old * sig_old * up_old).astype(jnp.bfloat16)
    d_gate = (d_act * up_old * sig_old * (1.0 + gate_old * (1.0 - sig_old))).astype(jnp.bfloat16)
    d_up = (d_act * gate_old * sig_old).astype(jnp.bfloat16)
    layer_out = (fresh.astype(jnp.float32) + jnp.dot(act_new, down_weight, preferred_element_type=jnp.float32)).astype(jnp.bfloat16)
    back = jnp.dot(d_gate, jnp.transpose(gate_weight), preferred_element_type=jnp.float32) + jnp.dot(d_up, jnp.transpose(up_weight), preferred_element_type=jnp.float32)
    input_grad = (incoming.astype(jnp.float32) + back).astype(jnp.bfloat16)
    grad_gate = jnp.dot(jnp.transpose(stored), d_gate, preferred_element_type=jnp.float32).astype(jnp.bfloat16)
    grad_up = jnp.dot(jnp.transpose(stored), d_up, preferred_element_type=jnp.float32).astype(jnp.bfloat16)
    grad_down = jnp.dot(jnp.transpose(act_old), incoming, preferred_element_type=jnp.float32).astype(jnp.bfloat16)
    return layer_out, input_grad, grad_gate, grad_up, grad_down


def reference(fwd_in, bwd_in, cotangent, w_gate, w_up, w_down):
    first = section_work(fwd_in[0], bwd_in[0], cotangent[0], w_gate[0], w_up[0], w_down[0])
    second = section_work(fwd_in[1], bwd_in[1], cotangent[1], w_gate[1], w_up[1], w_down[1])
    next_inputs = jnp.stack([second[0], first[0]])
    next_grads = jnp.stack([second[1], first[1]])
    grad_gate = jnp.stack([first[2], second[2]])
    grad_up = jnp.stack([first[3], second[3]])
    grad_down = jnp.stack([first[4], second[4]])
    return next_inputs, next_grads, grad_gate, grad_up, grad_down
```

```python
import functools

import jax
import jax.numpy as jnp
from jax import lax
from jax.experimental import pallas as pl
from jax.experimental.pallas import tpu as pltpu
from jax.sharding import PartitionSpec as P

MESH = pl.DeviceIdType.MESH
BF = jnp.bfloat16
F32 = jnp.float32
T = 384
B = 48
DW = 512
H = 896


def dot(left, right):
    return lax.dot_general(left, right, (((1,), (0,)), ((), ())), preferred_element_type=F32)


def dot_nt(left, right):
    return lax.dot_general(left, right, (((1,), (1,)), ((), ())), preferred_element_type=F32)


def tiles(width, step, body):
    whole = width // step

    @pl.loop(0, whole)
    def _(i):
        body(pl.ds(pl.multiple_of(i * step, step), step))

    if width % step:
        body(pl.ds(whole * step, width % step))


def kernel(
    x_new, x_old, x_cot, wg, wu, wd,
    o_next, o_grad, o_gg, o_gu, o_gd,
    G, WgH, WuH, WdH, WgX, WuX, WdX,
    PS, RL, PL, AD, AR, KS, XS, XR,
    A, TT, OP, ZS, RP, RM, LC, ES, ED, PM, ST, GG, GD,
    wsem, zr_s, zr_r, zl_s, zl_r, gs_s, gs_r, wx_s, wx_r,
    rs_s, rs_r, cy_s, cy_r, cr_s, cr_r, cx_s, cx_r, cs_s, cs_r,
    dp_s, dp_r, dm_s, dm_r, e_s, e_r, osem,
):
    s = lax.axis_index("section")
    r = lax.axis_index("row")
    c = lax.axis_index("col")
    y, xh, k = r // 4, (r // 2) % 2, r % 2
    xo = 1 - xh
    q = y * 2 + xh
    sib = {"row": r + 1 - 2 * k}
    yp = {"row": ((y + 1) % 4) * 4 + xh * 2 + k}
    ym = {"row": ((y + 3) % 4) * 4 + xh * 2 + k}
    xp = {"row": y * 4 + xo * 2 + k}
    zp = {"col": (c + 1) % 8}
    zm = {"col": (c + 7) % 8}
    far = [{"section": 1 - s, "row": (r + j) % 16} for j in range(16)]

    barrier = pltpu.get_barrier_semaphore()
    partners = [sib, yp, ym, xp, zp, zm] + far
    for d in partners:
        pl.semaphore_signal(barrier, inc=1, device_id=d, device_id_type=MESH)

    mine = pl.multiple_of(k * H, 128)
    other = pl.multiple_of((1 - k) * H, 128)
    loads = []

    def load(src, dst):
        cp = pltpu.make_async_copy(src, dst, wsem.at[len(loads)])
        cp.start()
        loads.append(cp)

    load(wg.at[:, pl.ds(mine, H)], WgH.at[0])
    load(wu.at[:, pl.ds(mine, H)], WuH.at[0])
    load(wd.at[pl.ds(mine, H), :], WdH.at[0])
    load(wg.at[:, pl.ds(other, H)], WgH.at[1])
    load(wu.at[:, pl.ds(other, H)], WuH.at[1])
    load(wd.at[pl.ds(other, H), :], WdH.at[1])

    def rows(block):
        return pl.ds(pl.multiple_of(lax.rem(block + 16, 8) * B, 16), B)

    sent = []

    def send(src, dst, ssem, rsem, to):
        cp = pltpu.make_async_remote_copy(
            src_ref=src, dst_ref=dst, send_sem=ssem, recv_sem=rsem, device_id=to, device_id_type=MESH
        )
        cp.start()
        sent.append(cp)
        return cp

    def got(ref, ssem, rsem):
        pltpu.make_async_remote_copy(
            src_ref=ref, dst_ref=ref, send_sem=ssem, recv_sem=rsem, device_id=sib, device_id_type=MESH
        ).wait_recv()

    xs = (x_new, x_old, x_cot)
    for a in range(3):
        G[a, 0, rows(c), :] = xs[a][...]

    pl.semaphore_wait(barrier, len(partners))

    hops_r = (4, 3, 4)
    hops_l = (3, 4, 3)

    def z_right(a, i):
        ref = G.at[a, 0, rows(c - i), :]
        send(ref, ref, zr_s.at[a, i], zr_r.at[a, i], zp)

    def z_left(a, i):
        ref = G.at[a, 0, rows(c + i), :]
        send(ref, ref, zl_s.at[a, i], zl_r.at[a, i], zm)

    def z_step(a, i):
        if i < hops_r[a]:
            if i > 0:
                got(G.at[a, 0, rows(c - i), :], zr_s.at[a, i - 1], zr_r.at[a, i - 1])
            z_right(a, i)
        elif i == hops_r[a]:
            got(G.at[a, 0, rows(c - i), :], zr_s.at[a, i - 1], zr_r.at[a, i - 1])
        if i < hops_l[a]:
            if i > 0:
                got(G.at[a, 0, rows(c + i), :], zl_s.at[a, i - 1], zl_r.at[a, i - 1])
            z_left(a, i)
        elif i == hops_l[a]:
            got(G.at[a, 0, rows(c + i), :], zl_s.at[a, i - 1], zl_r.at[a, i - 1])

    def z_share(a):
        send(G.at[a, 0], G.at[a, 1], gs_s.at[a], gs_r.at[a], sib)

    def z_shared(a):
        got(G.at[a, 1], gs_s.at[a], gs_r.at[a])

    def stage1(a, w):
        if a == 4:
            def tile(cols):
                acc = dot_nt(G[2, 0], WdH[0, cols, :]) + dot_nt(G[2, 1], WdX[cols, :])
                PS[a, :, cols] = acc.astype(BF)
        else:
            own, theirs = ((WgH, WgX), (WuH, WuX))[a % 2]
            t = a // 2

            def tile(cols):
                acc = dot(G[t, 0], own[0, :, cols]) + dot(G[t, 1], theirs[:, cols])
                PS[a, :, cols] = acc.astype(BF)

        tiles(H, 256, tile)
        up, down, across = 2 * (y + 1), 2 * (y - 1), 2 * (y + 2)
        send(PS.at[a, rows(across), :], RL.at[a, 0], rs_s.at[a, 0], rs_r.at[a, 0], yp)
        send(PS.at[a, rows(across + 1), :], RL.at[a, 1], rs_s.at[a, 1], rs_r.at[a, 1], ym)
        send(PS.at[a, rows(up + 1), :], PL.at[a, 1], rs_s.at[a, 2], rs_r.at[a, 2], yp)
        send(PS.at[a, rows(down), :], PL.at[a, 0], rs_s.at[a, 3], rs_r.at[a, 3], ym)

    def stage2(a):
        up, down = 2 * (y + 1), 2 * (y - 1)
        got(RL.at[a, 0], rs_s.at[a, 0], rs_r.at[a, 0])
        AD[a, 0] = (PS[a, rows(up), :].astype(F32) + RL[a, 0].astype(F32)).astype(BF)
        send(AD.at[a, 0], AR.at[a, 0], rs_s.at[a, 4], rs_r.at[a, 4], yp)
        got(RL.at[a, 1], rs_s.at[a, 1], rs_r.at[a, 1])
        AD[a, 1] = (PS[a, rows(down + 1), :].astype(F32) + RL[a, 1].astype(F32)).astype(BF)
        send(AD.at[a, 1], AR.at[a, 1], rs_s.at[a, 5], rs_r.at[a, 5], ym)

    def stage3(a):
        got(PL.at[a, 1], rs_s.at[a, 2], rs_r.at[a, 2])
        got(PL.at[a, 0], rs_s.at[a, 3], rs_r.at[a, 3])
        got(AR.at[a, 0], rs_s.at[a, 4], rs_r.at[a, 4])
        got(AR.at[a, 1], rs_s.at[a, 5], rs_r.at[a, 5])

        def total(which):
            return (
                PS[a, rows(2 * y + which), :].astype(F32)
                + PL[a, which].astype(F32)
                + AR[a, which].astype(F32)
            )

        XS[a] = total(xo).astype(BF)
        send(XS.at[a], XR.at[a], rs_s.at[a, 6], rs_r.at[a, 6], xp)
        KS[a] = total(xh)

    def stage4(a):
        got(XR.at[a], rs_s.at[a, 6], rs_r.at[a, 6])

    def value(a, cols):
        return KS[a, :, cols] + XR[a, :, cols].astype(F32)

    def sigmoid(v):
        return 1.0 / (1.0 + jnp.exp(-v))

    def activate_new():
        def tile(cols):
            gate, up = value(0, cols), value(1, cols)
            A[0, 0, rows(q), cols] = (gate * sigmoid(gate) * up).astype(BF)

        tiles(H, 128, tile)

    def activate_old():
        def tile(cols):
            gate, up, d = value(2, cols), value(3, cols), value(4, cols)
            sg = sigmoid(gate)
            A[1, 0, rows(q), cols] = (d * up * sg * (1.0 + gate * (1.0 - sg))).astype(BF)
            A[2, 0, rows(q), cols] = (d * gate * sg).astype(BF)
            A[3, 0, rows(q), cols] = (gate * sg * up).astype(BF)

        tiles(H, 128, tile)

    def c1(b):
        ref = A.at[b, 0, rows(q), :]
        send(ref, ref, cx_s.at[b], cx_r.at[b], xp)
        send(ref, ref, cy_s.at[b, 0, xh], cy_r.at[b, 0, xh], yp)
        send(ref, ref, cy_s.at[b, 1, xh], cy_r.at[b, 1, xh], ym)

    def c2(b):
        ref = A.at[b, 0, rows(2 * y + xo), :]
        got(ref, cx_s.at[b], cx_r.at[b])
        send(ref, ref, cy_s.at[b, 0, xo], cy_r.at[b, 0, xo], yp)
        send(ref, ref, cy_s.at[b, 1, xo], cy_r.at[b, 1, xo], ym)

    def c3(b):
        ref = A.at[b, 0, rows(2 * (y - 1)), :]
        got(ref, cy_s.at[b, 0, 0], cy_r.at[b, 0, 0])
        send(ref, ref, cr_s.at[b, 0], cr_r.at[b, 0], yp)
        ref = A.at[b, 0, rows(2 * (y + 1) + 1), :]
        got(ref, cy_s.at[b, 1, 1], cy_r.at[b, 1, 1])
        send(ref, ref, cr_s.at[b, 1], cr_r.at[b, 1], ym)

    def c4(b):
        got(A.at[b, 0, rows(2 * (y - 1) + 1), :], cy_s.at[b, 0, 1], cy_r.at[b, 0, 1])
        got(A.at[b, 0, rows(2 * (y + 1)), :], cy_s.at[b, 1, 0], cy_r.at[b, 1, 0])
        got(A.at[b, 0, rows(2 * (y + 2)), :], cr_s.at[b, 0], cr_r.at[b, 0])
        got(A.at[b, 0, rows(2 * (y + 2) + 1), :], cr_s.at[b, 1], cr_r.at[b, 1])
        send(A.at[b, 0], A.at[b, 1], cs_s.at[b], cs_r.at[b], sib)

    def c5(b):
        got(A.at[b, 1], cs_s.at[b], cs_r.at[b])

    def part_out():
        def tile(cols):
            acc = dot(A[0, 0], WdH[0, :, cols]) + dot(A[0, 1], WdH[1, :, cols])
            TT[0, :, cols] = acc.astype(BF)

        tiles(DW, 256, tile)

    def part_grad():
        def tile(cols):
            acc = dot_nt(A[1, 0], WgH[0, cols, :]) + dot_nt(A[1, 1], WgH[1, cols, :])
            acc += dot_nt(A[2, 0], WuH[0, cols, :]) + dot_nt(A[2, 1], WuH[1, cols, :])
            TT[1, :, cols] = acc.astype(BF)

        tiles(DW, 256, tile)

    hops_p = (4, 3)
    hops_m = (3, 4)

    def z_order(e):
        def tile(cols):
            OP[e, :, cols] = dot(PM[...], TT[e, :, cols]).astype(BF)

        tiles(DW, 256, tile)

    def d_step(e, i):
        for n, sem_s, sem_r, land, to, sign, side in (
            (hops_p[e], dp_s, dp_r, RP, zp, 1, 0),
            (hops_m[e], dm_s, dm_r, RM, zm, -1, 1),
        ):
            if i >= n:
                continue
            here = rows(c + sign * (n - i))
            if i == 0:
                send(OP.at[e, here, :], land.at[e, i], sem_s.at[e, i], sem_r.at[e, i], to)
            else:
                got(land.at[e, i - 1], sem_s.at[e, i - 1], sem_r.at[e, i - 1])
                ZS[e, side, i - 1] = (
                    OP[e, here, :].astype(F32) + land[e, i - 1].astype(F32)
                ).astype(BF)
                send(ZS.at[e, side, i - 1], land.at[e, i], sem_s.at[e, i], sem_r.at[e, i], to)

    def d_last(e):
        n, m = hops_p[e], hops_m[e]
        got(RP.at[e, n - 1], dp_s.at[e, n - 1], dp_r.at[e, n - 1])
        got(RM.at[e, m - 1], dm_s.at[e, m - 1], dm_r.at[e, m - 1])
        kept = dot(PM[rows(c), :], G[0 if e == 0 else 2, 0])
        full = OP[e, rows(c), :].astype(F32) + RP[e, n - 1].astype(F32) + RM[e, m - 1].astype(F32)
        LC[e * B : (e + 1) * B, :] = (full + kept).astype(BF)

    outs = []

    def put(src, dst):
        cp = pltpu.make_async_copy(src, dst, osem.at[len(outs)])
        cp.start()
        outs.append(cp)

    def grad_in(b, h):
        def tile(cols):
            GG[b - 1, h, :, cols] = dot(ST[...], A[b, h, :, cols]).astype(BF)

        tiles(H, 256, tile)
        put(GG.at[b - 1, h], (o_gg, o_gu)[b - 1].at[:, pl.ds((mine, other)[h], H)])

    def grad_out(h):
        def tile(cols):
            GD[h, cols, :] = lax.dot_general(
                A[3, h, :, cols], G[2, 0], (((0,), (0,)), ((), ())), preferred_element_type=F32
            ).astype(BF)

        tiles(H, 256, tile)
        put(GD.at[h], o_gd.at[pl.ds((mine, other)[h], H), :])

    send(wg.at[:, pl.ds(other, H)], WgX, wx_s.at[0], wx_r.at[0], sib)
    send(wu.at[:, pl.ds(other, H)], WuX, wx_s.at[1], wx_r.at[1], sib)
    send(wd.at[pl.ds(other, H), :], WdX, wx_s.at[2], wx_r.at[2], sib)

    z_step(0, 0)
    z_step(0, 1)
    z_step(1, 0)
    z_step(0, 2)
    z_step(1, 1)
    z_step(0, 3)
    z_step(2, 0)
    z_step(0, 4)
    z_share(0)
    z_step(1, 2)
    z_step(2, 1)

    pi = lax.broadcasted_iota(jnp.int32, (T, T), 0)
    ti = lax.broadcasted_iota(jnp.int32, (T, T), 1)
    token = ((pi % B) // 3) * 24 + (pi // B) * 3 + pi % 3
    PM[...] = jnp.where(ti == token, 1.0, 0.0).astype(BF)

    for cp in loads[:3]:
        cp.wait()
    got(WgX, wx_s.at[0], wx_r.at[0])
    got(WuX, wx_s.at[1], wx_r.at[1])
    z_shared(0)
    stage1(0, 0)
    z_step(1, 3)
    z_step(2, 2)
    stage1(1, 0)
    z_step(1, 4)
    z_share(1)
    z_step(2, 3)
    stage2(0)
    z_step(2, 4)
    z_share(2)
    z_shared(1)
    stage1(2, 0)
    stage2(1)
    stage3(0)
    stage1(3, 0)
    stage2(2)
    stage3(1)
    stage4(0)
    got(WdX, wx_s.at[2], wx_r.at[2])
    z_shared(2)
    stage1(4, 0)
    stage4(1)
    activate_new()
    stage2(3)
    c1(0)
    stage3(2)
    stage2(4)
    c2(0)
    stage3(3)
    c3(0)
    stage4(2)
    stage3(4)
    ST[...] = jnp.transpose(G[1, 0])
    stage4(3)
    c4(0)
    stage4(4)
    activate_old()
    c1(1)
    c1(2)
    c2(1)
    c2(2)
    for cp in loads[3:]:
        cp.wait()
    c5(0)
    part_out()
    z_order(0)
    d_step(0, 0)
    c3(1)
    c3(2)
    c1(3)
    d_step(0, 1)
    c4(1)
    d_step(0, 2)
    c4(2)
    c2(3)
    c5(1)
    c5(2)
    part_grad()
    z_order(1)
    d_step(1, 0)
    c3(3)
    d_step(0, 3)
    grad_in(1, 0)
    d_step(1, 1)
    c4(3)
    grad_in(1, 1)
    d_last(0)
    d_step(1, 2)
    grad_in(2, 0)
    d_step(1, 3)
    grad_in(2, 1)
    d_last(1)

    ri = lax.broadcasted_iota(jnp.int32, (256, 2 * B), 0)
    li = lax.broadcasted_iota(jnp.int32, (256, 2 * B), 1)
    sub = ri % 8
    spread = jnp.where((sub < 3) & (li == ((ri % 16) // 8) * B + (ri // 16) * 3 + sub), 1.0, 0.0)
    ES[...] = dot(spread.astype(BF), LC[...]).astype(BF)
    for j in range(16):
        there = pl.ds(pl.multiple_of(((r + j) % 16) * 16, 16), 16)
        here = pl.ds(pl.multiple_of(r * 16, 16), 16)
        send(ES.at[there, :], ED.at[here, :], e_s.at[j], e_r.at[j], far[j])

    c5(3)
    grad_out(0)
    grad_out(1)
    for j in range(16):
        got(ED.at[pl.ds(pl.multiple_of(((r + 16 - j) % 16) * 16, 16), 16), :], e_s.at[j], e_r.at[j])
    for j in range(16):
        tile = ED[j * 16 : j * 16 + 16, :]
        o_next[:, j * DW : (j + 1) * DW] = tile[0:3]
        o_grad[:, j * DW : (j + 1) * DW] = tile[8:11]
    for cp in outs:
        cp.wait()
    for cp in sent:
        cp.wait_send()


def body(fwd_in, bwd_in, cotangent, w_gate, w_up, w_down):
    vmem = pl.BlockSpec(memory_space=pltpu.VMEM)
    hbm = pl.BlockSpec(memory_space=pl.ANY)
    V = pltpu.VMEM
    D = pltpu.SemaphoreType.DMA
    scratch = [
        V((3, 2, T, DW), BF),
        V((2, DW, H), BF), V((2, DW, H), BF), V((2, H, DW), BF),
        V((DW, H), BF), V((DW, H), BF), V((H, DW), BF),
        V((5, T, H), BF),
        V((5, 2, B, H), BF), V((5, 2, B, H), BF), V((5, 2, B, H), BF), V((5, 2, B, H), BF),
        V((5, B, H), F32), V((5, B, H), BF), V((5, B, H), BF),
        V((4, 2, T, H), BF),
        V((2, T, DW), BF), V((2, T, DW), BF),
        V((2, 2, 3, B, DW), BF), V((2, 4, B, DW), BF), V((2, 4, B, DW), BF),
        V((2 * B, DW), BF), V((256, DW), BF), V((256, DW), BF),
        V((T, T), BF), V((DW, T), BF),
        V((2, 2, DW, H), BF), V((2, H, DW), BF),
        D((6,)), D((3, 4)), D((3, 4)), D((3, 4)), D((3, 4)), D((3,)), D((3,)), D((3,)), D((3,)),
        D((5, 7)), D((5, 7)), D((4, 2, 2)), D((4, 2, 2)), D((4, 2)), D((4, 2)),
        D((4,)), D((4,)), D((4,)), D((4,)),
        D((2, 4)), D((2, 4)), D((2, 4)), D((2, 4)), D((16,)), D((16,)), D((6,)),
    ]
    n, g, gg, gu, gd = pl.pallas_call(
        kernel,
        out_shape=(
            jax.ShapeDtypeStruct((3, 16 * DW), BF),
            jax.ShapeDtypeStruct((3, 16 * DW), BF),
            jax.ShapeDtypeStruct((DW, 2 * H), BF),
            jax.ShapeDtypeStruct((DW, 2 * H), BF),
            jax.ShapeDtypeStruct((2 * H, DW), BF),
        ),
        in_specs=[vmem] * 3 + [hbm] * 3,
        out_specs=(vmem, vmem, hbm, hbm, hbm),
        scratch_shapes=scratch,
        compiler_params=pltpu.CompilerParams(
            collective_id=0, has_side_effects=True, vmem_limit_bytes=56 * 2**20
        ),
        cost_estimate=pl.CostEstimate(flops=8 * 10**9, bytes_accessed=12 * 10**6, transcendentals=0),
        name="relay",
    )(fwd_in[0], bwd_in[0], cotangent[0], w_gate[0], w_up[0], w_down[0])
    return n[None], g[None], gg[None], gu[None], gd[None]


def solution(mesh):
    in_specs = (
        P("section", "col", "row"),
        P("section", "col", "row"),
        P("section", "col", "row"),
        P("section", "row", "col"),
        P("section", "row", "col"),
        P("section", "col", "row"),
    )
    out_specs = (
        P("section", ("row", "col"), None),
        P("section", ("row", "col"), None),
        P("section", "row", "col"),
        P("section", "row", "col"),
        P("section", "col", "row"),
    )
    return jax.shard_map(body, mesh=mesh, in_specs=in_specs, out_specs=out_specs, check_vma=False)
```

```python
import functools

import jax
import jax.numpy as jnp
from jax import lax
from jax.experimental import pallas as pl
from jax.experimental.pallas import tpu as pltpu
from jax.sharding import PartitionSpec as P

MESH = pl.DeviceIdType.MESH
BF = jnp.bfloat16
F32 = jnp.float32
T = 384
B = 48
DW = 512
H = 896
LOW, HIGH = pl.ds(0, 512), pl.ds(512, 384)
SUM_X = {1: 0, 3: 1}
GATHER_X = (2, 3)


def dot(left, right):
    return lax.dot_general(left, right, (((1,), (0,)), ((), ())), preferred_element_type=F32)


def dot_nt(left, right):
    return lax.dot_general(left, right, (((1,), (1,)), ((), ())), preferred_element_type=F32)


def tiles(width, step, body):
    whole = width // step

    @pl.loop(0, whole)
    def _(i):
        body(pl.ds(pl.multiple_of(i * step, step), step))

    if width % step:
        body(pl.ds(whole * step, width % step))


def kernel(
    x_new, x_old, x_cot, wg, wu, wd,
    o_seen, o_gg, o_gu, o_gd,
    G, WgH, WuH, WdH, WgX, WuX, WdX,
    PS, RL, PL, AD, AR, KS, XS, XR, XQ, SX,
    A, TT, AC, OP, ZS, RD, RES, LS, ES, ED, PM, SP, ST, GG, GD,
    wsem, xsem, z_s, z_r, gs_s, gs_r, wx_s, wx_r,
    rs_s, rs_r, cy_s, cy_r, cr_s, cr_r, cx_s, cx_r, cs_s, cs_r,
    d_s, d_r, e_s, e_r, osem, row_sem,
):
    s = lax.axis_index("section")
    r = lax.axis_index("row")
    c = lax.axis_index("col")
    y, xh, k = r // 4, (r // 2) % 2, r % 2
    xo = 1 - xh
    q = y * 2 + xh
    sib = {"row": r + 1 - 2 * k}
    yp = {"row": ((y + 1) % 4) * 4 + xh * 2 + k}
    ym = {"row": ((y + 3) % 4) * 4 + xh * 2 + k}
    xp = {"row": y * 4 + xo * 2 + k}
    zat = {d: {"col": (c + d + 8) % 8} for d in (1, -1, 2, -2)}
    far = [{"section": 1 - s, "row": (r + j) % 16} for j in range(16)]

    barrier = pltpu.get_barrier_semaphore()
    partners = [sib, yp, ym, xp, {"section": 1 - s}] + list(zat.values())
    for d in partners:
        pl.semaphore_signal(barrier, inc=1, device_id=d, device_id_type=MESH)

    mine = pl.multiple_of(k * H, 128)
    other = pl.multiple_of((1 - k) * H, 128)
    loads = []

    def load(src, dst):
        cp = pltpu.make_async_copy(src, dst, wsem.at[len(loads)])
        cp.start()
        loads.append(cp)

    def load_early():
        load(wg.at[:, pl.ds(mine, H)], WgH.at[0])
        load(wu.at[:, pl.ds(mine, H)], WuH.at[0])

    def load_down():
        load(wd.at[pl.ds(mine, H), :], WdH.at[0])
        send(wd.at[pl.ds(other, H), :], WdX, wx_s.at[2], wx_r.at[2], sib)

    def load_late():
        load(wg.at[:, pl.ds(other, H)], WgH.at[1])
        load(wu.at[:, pl.ds(other, H)], WuH.at[1])
        load(wd.at[pl.ds(other, H), :], WdH.at[1])

    def rows(block):
        return pl.ds(pl.multiple_of(lax.rem(block + 16, 8) * B, 16), B)

    sent = []

    def send(src, dst, ssem, rsem, to):
        cp = pltpu.make_async_remote_copy(
            src_ref=src, dst_ref=dst, send_sem=ssem, recv_sem=rsem, device_id=to, device_id_type=MESH
        )
        cp.start()
        sent.append(cp)
        return cp

    def got(ref, ssem, rsem):
        pltpu.make_async_remote_copy(
            src_ref=ref, dst_ref=ref, send_sem=ssem, recv_sem=rsem, device_id=sib, device_id_type=MESH
        ).wait_recv()

    xs = (x_new, x_old, x_cot)
    kept = []
    for a in range(3):
        cp = pltpu.make_async_copy(xs[a], G.at[a, 0, rows(c), :], xsem.at[a])
        cp.start()
        kept.append(cp)
    load_early()
    pl.semaphore_wait(barrier, len(partners))

    def z_send(a, src, block, j, to):
        ref = G.at[a, 0, rows(block), :]
        send(ref if src is None else src, ref, z_s.at[a, j], z_r.at[a, j], zat[to])

    def z_got(a, block, j):
        ref = G.at[a, 0, rows(block), :]
        got(ref, z_s.at[a, j], z_r.at[a, j])
        send(ref, G.at[a, 1, rows(block), :], gs_s.at[a, j], gs_r.at[a, j], sib)

    def z1(a):
        z_send(a, xs[a], c, 2, 2)
        z_send(a, xs[a], c, 3, -2)
        z_send(a, xs[a], c, 0, 1)
        z_send(a, xs[a], c, 1, -1)
        send(xs[a], G.at[a, 1, rows(c), :], gs_s.at[a, 7], gs_r.at[a, 7], sib)

    def z_near(a):
        z_got(a, c - 1, 0)
        z_got(a, c + 1, 1)

    def z2(a):
        z_got(a, c - 2, 2)
        if a % 2 == 0:
            z_send(a, None, c - 2, 6, 2)
        z_send(a, None, c - 2, 4, 1)
        z_got(a, c + 2, 3)
        if a % 2 == 1:
            z_send(a, None, c + 2, 6, -2)
        z_send(a, None, c + 2, 5, -1)

    def z3(a):
        z_got(a, c - 3, 4)
        z_got(a, c + 3, 5)
        z_got(a, c + 4, 6)

    def z_shared(a):
        kept[a].wait()
        for j in range(8):
            got(G.at[a, 1, rows(c), :], gs_s.at[a, j], gs_r.at[a, j])

    def stage1(a):
        if a == 4:
            def tile(cols):
                acc = dot_nt(G[2, 0], WdH[0, cols, :]) + dot_nt(G[2, 1], WdX[cols, :])
                PS[a, :, cols] = acc.astype(BF)
        else:
            own, theirs = ((WgH, WgX), (WuH, WuX))[a % 2]
            t = a // 2

            def tile(cols):
                acc = dot(G[t, 0], own[0, :, cols]) + dot(G[t, 1], theirs[:, cols])
                PS[a, :, cols] = acc.astype(BF)

        tiles(H, 256, tile)
        up, down, across = 2 * (y + 1), 2 * (y - 1), 2 * (y + 2)
        if a in SUM_X:
            for j, block in enumerate((across, up, down, 2 * y)):
                send(PS.at[a, rows(block + xo), :], XQ.at[SUM_X[a], j], rs_s.at[a, j], rs_r.at[a, j], xp)
            return
        send(PS.at[a, rows(across), :], RL.at[a, 0], rs_s.at[a, 0], rs_r.at[a, 0], yp)
        send(PS.at[a, rows(across + 1), :], RL.at[a, 1], rs_s.at[a, 1], rs_r.at[a, 1], ym)
        send(PS.at[a, rows(up + 1), :], PL.at[a, 1], rs_s.at[a, 2], rs_r.at[a, 2], yp)
        send(PS.at[a, rows(down), :], PL.at[a, 0], rs_s.at[a, 3], rs_r.at[a, 3], ym)

    def crossed(a, j, block):
        return PS[a, rows(block + xh), :].astype(F32) + XQ[SUM_X[a], j].astype(F32)

    def stage2x(a):
        n = SUM_X[a]
        got(XQ.at[n, 0], rs_s.at[a, 0], rs_r.at[a, 0])
        SX[n, 0] = crossed(a, 0, 2 * (y + 2)).astype(BF)
        send(SX.at[n, 0, :, LOW], RL.at[a, 0, :, LOW], rs_s.at[a, 4], rs_r.at[a, 4], yp)
        send(SX.at[n, 0, :, HIGH], RL.at[a, 0, :, HIGH], rs_s.at[a, 5], rs_r.at[a, 5], ym)
        got(XQ.at[n, 1], rs_s.at[a, 1], rs_r.at[a, 1])
        SX[n, 1] = crossed(a, 1, 2 * (y + 1)).astype(BF)
        send(SX.at[n, 1, :, HIGH], PL.at[a, 0, :, HIGH], rs_s.at[a, 6], rs_r.at[a, 6], yp)
        got(XQ.at[n, 2], rs_s.at[a, 2], rs_r.at[a, 2])
        SX[n, 2] = crossed(a, 2, 2 * (y - 1)).astype(BF)
        send(SX.at[n, 2, :, LOW], PL.at[a, 0, :, LOW], rs_s.at[a, 7], rs_r.at[a, 7], ym)
        got(XQ.at[n, 3], rs_s.at[a, 3], rs_r.at[a, 3])
        KS[a] = crossed(a, 3, 2 * y)

    def stage3x(a):
        n = SUM_X[a]
        got(RL.at[a, 0, :, LOW], rs_s.at[a, 4], rs_r.at[a, 4])
        full = PS[a, rows(2 * (y + 1) + xh), LOW].astype(F32) + XQ[n, 1, :, LOW].astype(F32)
        AD[a, 0, :, LOW] = (full + RL[a, 0, :, LOW].astype(F32)).astype(BF)
        send(AD.at[a, 0, :, LOW], AR.at[a, 0, :, LOW], rs_s.at[a, 8], rs_r.at[a, 8], yp)
        got(RL.at[a, 0, :, HIGH], rs_s.at[a, 5], rs_r.at[a, 5])
        full = PS[a, rows(2 * (y - 1) + xh), HIGH].astype(F32) + XQ[n, 2, :, HIGH].astype(F32)
        AD[a, 0, :, HIGH] = (full + RL[a, 0, :, HIGH].astype(F32)).astype(BF)
        send(AD.at[a, 0, :, HIGH], AR.at[a, 0, :, HIGH], rs_s.at[a, 9], rs_r.at[a, 9], ym)

    def stage4x(a):
        for j, cols in ((6, HIGH), (7, LOW), (8, LOW), (9, HIGH)):
            got(RL.at[a, 0, :, cols], rs_s.at[a, j], rs_r.at[a, j])

    def stage2(a):
        up, down = 2 * (y + 1), 2 * (y - 1)
        got(RL.at[a, 0], rs_s.at[a, 0], rs_r.at[a, 0])
        AD[a, 0] = (PS[a, rows(up), :].astype(F32) + RL[a, 0].astype(F32)).astype(BF)
        send(AD.at[a, 0], AR.at[a, 0], rs_s.at[a, 4], rs_r.at[a, 4], yp)
        got(RL.at[a, 1], rs_s.at[a, 1], rs_r.at[a, 1])
        AD[a, 1] = (PS[a, rows(down + 1), :].astype(F32) + RL[a, 1].astype(F32)).astype(BF)
        send(AD.at[a, 1], AR.at[a, 1], rs_s.at[a, 5], rs_r.at[a, 5], ym)

    def stage3(a):
        got(PL.at[a, 1], rs_s.at[a, 2], rs_r.at[a, 2])
        got(PL.at[a, 0], rs_s.at[a, 3], rs_r.at[a, 3])
        got(AR.at[a, 0], rs_s.at[a, 4], rs_r.at[a, 4])
        got(AR.at[a, 1], rs_s.at[a, 5], rs_r.at[a, 5])

        def total(which):
            return (
                PS[a, rows(2 * y + which), :].astype(F32)
                + PL[a, which].astype(F32)
                + AR[a, which].astype(F32)
            )

        XS[a] = total(xo).astype(BF)
        send(XS.at[a], XR.at[a], rs_s.at[a, 6], rs_r.at[a, 6], xp)
        KS[a] = total(xh)

    def stage4(a):
        got(XR.at[a], rs_s.at[a, 6], rs_r.at[a, 6])

    def value(a, cols):
        if a in SUM_X:
            return KS[a, :, cols] + PL[a, 0, :, cols].astype(F32) + AR[a, 0, :, cols].astype(F32)
        return KS[a, :, cols] + XR[a, :, cols].astype(F32)

    def sigmoid(v):
        return 1.0 / (1.0 + jnp.exp(-v))

    def activate_new():
        def tile(cols):
            gate, up = value(0, cols), value(1, cols)
            A[0, 0, rows(q), cols] = (gate * sigmoid(gate) * up).astype(BF)

        tiles(H, 128, tile)

    def activate_old():
        def tile(cols):
            gate, up, d = value(2, cols), value(3, cols), value(4, cols)
            sg = sigmoid(gate)
            A[1, 0, rows(q), cols] = (d * up * sg * (1.0 + gate * (1.0 - sg))).astype(BF)
            A[2, 0, rows(q), cols] = (d * gate * sg).astype(BF)
            A[3, 0, rows(q), cols] = (gate * sg * up).astype(BF)

        tiles(H, 128, tile)

    def share(b, ref, block, j):
        send(ref, A.at[b, 1, rows(block), :], cs_s.at[b, j], cs_r.at[b, j], sib)

    def c1(b):
        ref = A.at[b, 0, rows(q), :]
        send(ref, ref, cx_s.at[b, 0], cx_r.at[b, 0], xp)
        send(ref, ref, cy_s.at[b, 0, xh], cy_r.at[b, 0, xh], yp)
        send(ref, ref, cy_s.at[b, 1, xh], cy_r.at[b, 1, xh], ym)
        share(b, ref, q, 0)

    def c2(b):
        block = 2 * y + xo
        ref = A.at[b, 0, rows(block), :]
        got(ref, cx_s.at[b, 0], cx_r.at[b, 0])
        send(ref, ref, cy_s.at[b, 0, xo], cy_r.at[b, 0, xo], yp)
        send(ref, ref, cy_s.at[b, 1, xo], cy_r.at[b, 1, xo], ym)
        share(b, ref, block, 1)

    def c3(b):
        block = 2 * (y - 1)
        ref = A.at[b, 0, rows(block), :]
        got(ref, cy_s.at[b, 0, 0], cy_r.at[b, 0, 0])
        send(ref, ref, cr_s.at[b, 0], cr_r.at[b, 0], yp)
        share(b, ref, block, 2)
        block = 2 * (y + 1) + 1
        ref = A.at[b, 0, rows(block), :]
        got(ref, cy_s.at[b, 1, 1], cy_r.at[b, 1, 1])
        send(ref, ref, cr_s.at[b, 1], cr_r.at[b, 1], ym)
        share(b, ref, block, 3)

    def c4(b):
        for j, (block, sem_s, sem_r) in enumerate((
            (2 * (y - 1) + 1, cy_s.at[b, 0, 1], cy_r.at[b, 0, 1]),
            (2 * (y + 1), cy_s.at[b, 1, 0], cy_r.at[b, 1, 0]),
            (2 * (y + 2), cr_s.at[b, 0], cr_r.at[b, 0]),
            (2 * (y + 2) + 1, cr_s.at[b, 1], cr_r.at[b, 1]),
        )):
            ref = A.at[b, 0, rows(block), :]
            got(ref, sem_s, sem_r)
            share(b, ref, block, 4 + j)

    def c1x(b):
        ref = A.at[b, 0, rows(q), :]
        send(ref, ref, cy_s.at[b, 0, 0], cy_r.at[b, 0, 0], yp)
        send(ref, ref, cy_s.at[b, 1, 0], cy_r.at[b, 1, 0], ym)
        send(ref, ref, cx_s.at[b, 0], cx_r.at[b, 0], xp)
        share(b, ref, q, 0)

    def c2x(b):
        for side, sign, cols, to in ((0, -1, LOW, yp), (1, 1, HIGH, ym)):
            block = 2 * (y + sign) + xh
            ref = A.at[b, 0, rows(block), :]
            got(ref, cy_s.at[b, side, 0], cy_r.at[b, side, 0])
            part = A.at[b, 0, rows(block), cols]
            send(part, part, cr_s.at[b, side], cr_r.at[b, side], to)
            send(ref, ref, cx_s.at[b, 1 + side], cx_r.at[b, 1 + side], xp)
            share(b, ref, block, 1 + side)

    def c3x(b):
        block = 2 * (y + 2) + xh
        ref = A.at[b, 0, rows(block), :]
        got(A.at[b, 0, rows(block), LOW], cr_s.at[b, 0], cr_r.at[b, 0])
        got(A.at[b, 0, rows(block), HIGH], cr_s.at[b, 1], cr_r.at[b, 1])
        send(ref, ref, cx_s.at[b, 3], cx_r.at[b, 3], xp)
        share(b, ref, block, 3)

    def c4x(b):
        for j, place in enumerate((y, y - 1, y + 1, y + 2)):
            ref = A.at[b, 0, rows(2 * place + xo), :]
            got(ref, cx_s.at[b, j], cx_r.at[b, j])
            share(b, ref, 2 * place + xo, 4 + j)

    def c5(b):
        for j in range(8):
            got(A.at[b, 1, rows(q), :], cs_s.at[b, j], cs_r.at[b, j])

    def part_out():
        def tile(cols):
            acc = dot(A[0, 0], WdH[0, :, cols]) + dot(A[0, 1], WdH[1, :, cols])
            TT[0, :, cols] = acc.astype(BF)

        tiles(DW, 256, tile)

    def part_gate():
        def tile(cols):
            AC[:, cols] = dot_nt(A[1, 0], WgH[0, cols, :]) + dot_nt(A[1, 1], WgH[1, cols, :])

        tiles(DW, 256, tile)

    def part_grad():
        def tile(cols):
            acc = dot_nt(A[2, 0], WuH[0, cols, :]) + dot_nt(A[2, 1], WuH[1, cols, :])
            TT[1, :, cols] = (AC[:, cols] + acc).astype(BF)

        tiles(DW, 256, tile)

    def z_order(e):
        def tile(cols):
            OP[e, :, cols] = dot(PM[...], TT[e, :, cols]).astype(BF)

        tiles(DW, 256, tile)

    def d1(e):
        def out(block, side, j, to):
            send(OP.at[e, rows(block), :], RD.at[e, side, j], d_s.at[e, side, j], d_r.at[e, side, j], zat[to])

        far_side = e % 2
        sign = 1 if far_side == 0 else -1
        out(c + 4, far_side, 3, 2 * sign)
        out(c + 3, 0, 2, 1)
        out(c - 3, 1, 2, -1)
        out(c + 1, 0, 0, 1)
        out(c - 1, 1, 0, -1)

    def d_got(e, side, j):
        got(RD.at[e, side, j], d_s.at[e, side, j], d_r.at[e, side, j])
        return RD[e, side, j].astype(F32)

    def d2(e):
        for side, sign in ((0, 1), (1, -1)):
            acc = OP[e, rows(c + 2 * sign), :].astype(F32) + d_got(e, side, 2)
            if side == e % 2:
                acc += d_got(e, side, 3)
            ZS[e, side] = acc.astype(BF)
            send(ZS.at[e, side], RD.at[e, side, 1], d_s.at[e, side, 1], d_r.at[e, side, 1], zat[2 * sign])

    def residual(e):
        RES[e] = dot(PM[rows(c), :], G[0 if e == 0 else 2, 0])

    def d_last(e):
        full = OP[e, rows(c), :].astype(F32)
        full += d_got(e, 0, 0) + d_got(e, 1, 0) + d_got(e, 0, 1) + d_got(e, 1, 1)
        full = (full + RES[e]).astype(BF)
        for j in range(4):
            LS[e, j * B : (j + 1) * B, :] = full[:, j * 128 : (j + 1) * 128]

    def e_send(e):
        ES[e] = dot(SP[...], LS[e]).astype(BF)
        for j in range(16):
            there = pl.ds(pl.multiple_of(((r + j) % 16) * 16, 16), 16)
            here = pl.ds(pl.multiple_of(r * 16, 16), 16)
            send(ES.at[e, there, :], ED.at[e, here, :], e_s.at[e, j], e_r.at[e, j], far[j])

    def e_wait(e):
        for j in range(16):
            got(ED.at[e, pl.ds(0, 16), :], e_s.at[e, j], e_r.at[e, j])

    outs = []

    def put(src, dst):
        cp = pltpu.make_async_copy(src, dst, osem.at[len(outs)])
        cp.start()
        outs.append(cp)

    def grad_in(b, h):
        def tile(cols):
            GG[b - 1, h, :, cols] = dot(ST[...], A[b, h, :, cols]).astype(BF)

        tiles(H, 256, tile)
        put(GG.at[b - 1, h], (o_gg, o_gu)[b - 1].at[:, pl.ds((mine, other)[h], H)])

    def grad_out(h):
        def tile(cols):
            GD[h, cols, :] = lax.dot_general(
                A[3, h, :, cols], G[2, 0], (((0,), (0,)), ((), ())), preferred_element_type=F32
            ).astype(BF)

        tiles(H, 256, tile)
        put(GD.at[h], o_gd.at[pl.ds((mine, other)[h], H), :])

    z1(0)
    z1(1)
    send(wg.at[:, pl.ds(other, H)], WgX, wx_s.at[0], wx_r.at[0], sib)
    send(wu.at[:, pl.ds(other, H)], WuX, wx_s.at[1], wx_r.at[1], sib)
    z_near(0)
    z2(0)
    z1(2)
    load_down()
    z_near(1)
    z2(1)
    z3(0)
    loads[1].wait()
    got(WuX, wx_s.at[1], wx_r.at[1])
    z_shared(0)
    stage1(1)
    z_near(2)
    z2(2)
    loads[0].wait()
    got(WgX, wx_s.at[0], wx_r.at[0])
    stage1(0)
    z3(1)
    z_shared(1)
    stage1(3)
    z3(2)
    load_late()
    stage2(0)
    stage2x(1)
    stage1(2)
    loads[2].wait()
    got(WdX, wx_s.at[2], wx_r.at[2])
    z_shared(2)
    stage1(4)
    stage3(0)
    stage3x(1)
    stage2x(3)
    stage2(2)
    stage4(0)
    stage4x(1)
    activate_new()
    c1(0)
    stage2(4)
    stage3(2)
    stage3x(3)
    c2(0)
    stage3(4)
    c3(0)

    pi = lax.broadcasted_iota(jnp.int32, (T, T), 0)
    ti = lax.broadcasted_iota(jnp.int32, (T, T), 1)
    token = ((pi % B) // 3) * 24 + (pi // B) * 3 + pi % 3
    PM[...] = jnp.where(ti == token, 1.0, 0.0).astype(BF)
    ST[...] = jnp.transpose(G[1, 0])

    stage4(2)
    stage4x(3)
    stage4(4)
    activate_old()
    c1x(2)
    c1(1)
    c4(0)
    c2x(2)
    c2(1)
    for cp in loads[3:]:
        cp.wait()
    c3x(2)
    c3(1)
    c5(0)
    pl.semaphore_signal(row_sem, inc=1, device_id={"section": 1 - s}, device_id_type=MESH)
    part_out()
    z_order(0)
    d1(0)
    c4(1)
    c1x(3)
    residual(0)
    residual(1)
    c4x(2)
    c5(1)
    part_gate()
    c2x(3)
    d2(0)
    c5(2)
    part_grad()
    z_order(1)
    d1(1)
    d_last(0)

    ri = lax.broadcasted_iota(jnp.int32, (256, 4 * B), 0)
    li = lax.broadcasted_iota(jnp.int32, (256, 4 * B), 1)
    sub = ri % 16
    hit = (sub < 12) & (li // B == sub // 3) & (li % B == (ri // 16) * 3 + sub % 3)
    SP[...] = jnp.where(hit, 1.0, 0.0).astype(BF)

    pl.semaphore_wait(row_sem, 1)
    e_send(0)
    c3x(3)
    grad_in(1, 0)
    d2(1)
    c4x(3)
    grad_in(1, 1)
    grad_in(2, 0)
    d_last(1)
    e_send(1)
    grad_in(2, 1)
    c5(3)
    grad_out(0)
    grad_out(1)
    e_wait(0)
    e_wait(1)
    o_seen[...] = ED[...]
    for cp in outs:
        cp.wait()
    for cp in sent:
        cp.wait_send()


def finish(seen, gg, gu, gd, o_next, o_grad, o_gg, o_gu, o_gd, sem):
    copies = []
    for i, (src, dst) in enumerate(((gg, o_gg), (gu, o_gu), (gd, o_gd))):
        part = src.shape[0] // 4
        for j in range(4):
            here = pl.ds(j * part, part)
            cp = pltpu.make_async_copy(src.at[here, :], dst.at[0, here, :], sem.at[i, j])
            cp.start()
            copies.append(cp)
    for e, dst in enumerate((o_next, o_grad)):
        for j in range(16):
            for i in range(4):
                at = j * DW + i * 128
                dst[0, :, at : at + 128] = seen[e, j * 16 + i * 3 : j * 16 + i * 3 + 3, :]
    for cp in copies:
        cp.wait()


def body(fwd_in, bwd_in, cotangent, w_gate, w_up, w_down):
    vmem = pl.BlockSpec(memory_space=pltpu.VMEM)
    hbm = pl.BlockSpec(memory_space=pltpu.HBM)
    V = pltpu.VMEM
    D = pltpu.SemaphoreType.DMA
    scratch = [
        V((3, 2, T, DW), BF),
        V((2, DW, H), BF), V((2, DW, H), BF), V((2, H, DW), BF),
        V((DW, H), BF), V((DW, H), BF), V((H, DW), BF),
        V((5, T, H), BF),
        V((5, 2, B, H), BF), V((5, 2, B, H), BF), V((5, 2, B, H), BF), V((5, 2, B, H), BF),
        V((5, B, H), F32), V((5, B, H), BF), V((5, B, H), BF),
        V((2, 4, B, H), BF), V((2, 3, B, H), BF),
        V((4, 2, T, H), BF),
        V((2, T, DW), BF), V((T, DW), F32), V((2, T, DW), BF),
        V((2, 2, B, DW), BF), V((2, 2, 4, B, DW), BF),
        V((2, B, DW), F32), V((2, 4 * B, 128), BF), V((2, 256, 128), BF), V((2, 256, 128), BF),
        V((T, T), BF), V((256, 4 * B), BF), V((DW, T), BF),
        V((2, 2, DW, H), BF), V((2, H, DW), BF),
        D((6,)), D((3,)), D((3, 7)), D((3, 7)), D((3, 8)), D((3, 8)), D((3,)), D((3,)),
        D((5, 10)), D((5, 10)), D((4, 2, 2)), D((4, 2, 2)), D((4, 2)), D((4, 2)),
        D((4, 4)), D((4, 4)), D((4, 8)), D((4, 8)),
        D((2, 2, 4)), D((2, 2, 4)), D((2, 16)), D((2, 16)), D((6,)), pltpu.SemaphoreType.REGULAR,
    ]
    seen, gg, gu, gd = pl.pallas_call(
        kernel,
        out_shape=(
            jax.ShapeDtypeStruct((2, 256, 128), BF),
            jax.ShapeDtypeStruct((DW, 2 * H), BF),
            jax.ShapeDtypeStruct((DW, 2 * H), BF),
            jax.ShapeDtypeStruct((2 * H, DW), BF),
        ),
        in_specs=[vmem] * 3 + [hbm] * 3,
        out_specs=(vmem, hbm, hbm, hbm),
        scratch_shapes=scratch,
        compiler_params=pltpu.CompilerParams(
            collective_id=0, has_side_effects=True, vmem_limit_bytes=50 * 2**20
        ),
        cost_estimate=pl.CostEstimate(flops=8 * 10**9, bytes_accessed=12 * 10**6, transcendentals=0),
        name="relay",
    )(fwd_in[0], bwd_in[0], cotangent[0], w_gate[0], w_up[0], w_down[0])
    return pl.pallas_call(
        finish,
        out_shape=(
            jax.ShapeDtypeStruct((1, 3, 16 * DW), BF),
            jax.ShapeDtypeStruct((1, 3, 16 * DW), BF),
            jax.ShapeDtypeStruct((1, DW, 2 * H), BF),
            jax.ShapeDtypeStruct((1, DW, 2 * H), BF),
            jax.ShapeDtypeStruct((1, 2 * H, DW), BF),
        ),
        in_specs=[vmem, hbm, hbm, hbm],
        out_specs=(vmem, vmem, hbm, hbm, hbm),
        scratch_shapes=[pltpu.SemaphoreType.DMA((3, 4))],
        compiler_params=pltpu.CompilerParams(vmem_limit_bytes=16 * 2**20),
        name="finish",
    )(seen, gg, gu, gd)


def solution(mesh):
    in_specs = (
        P("section", "col", "row"),
        P("section", "col", "row"),
        P("section", "col", "row"),
        P("section", "row", "col"),
        P("section", "row", "col"),
        P("section", "col", "row"),
    )
    out_specs = (
        P("section", ("row", "col"), None),
        P("section", ("row", "col"), None),
        P("section", "row", "col"),
        P("section", "row", "col"),
        P("section", "col", "row"),
    )
    return jax.shard_map(body, mesh=mesh, in_specs=in_specs, out_specs=out_specs, check_vma=False)
```

```python
import functools

import jax
import jax.numpy as jnp
from jax import lax
from jax.experimental import pallas as pl
from jax.experimental.pallas import tpu as pltpu
from jax.sharding import PartitionSpec as P

MESH = pl.DeviceIdType.MESH
BF = jnp.bfloat16
F32 = jnp.float32
T = 384
B = 48
DW = 512
H = 896
LOW, HIGH = pl.ds(0, 512), pl.ds(512, 384)
SUM_X = {1: 0, 3: 1}


def dot(left, right):
    return lax.dot_general(left, right, (((1,), (0,)), ((), ())), preferred_element_type=F32)


def dot_nt(left, right):
    return lax.dot_general(left, right, (((1,), (1,)), ((), ())), preferred_element_type=F32)


def tiles(width, step, body):
    whole = width // step

    @pl.loop(0, whole)
    def _(i):
        body(pl.ds(pl.multiple_of(i * step, step), step))

    if width % step:
        body(pl.ds(whole * step, width % step))


def kernel(
    x_new, x_old, x_cot, wg, wu, wd,
    o_seen, o_gg, o_gu, o_gd,
    G, WgH, WuH, WdH, WgX, WuX, WdX,
    PS, RL, PL, AD, AR, KS, XS, XR, XQ, SX,
    A, TT, AC, OP, ZS, RD, RES, LS, ES, ED, PM, SP, ST, GG, GD,
    wsem, xsem, z_s, z_r, gs_s, gs_r, wx_s, wx_r,
    rs_s, rs_r, cy_s, cy_r, cr_s, cr_r, cx_s, cx_r, cs_s, cs_r,
    d_s, d_r, e_s, e_r, osem, row_sem,
):
    s = lax.axis_index("section")
    r = lax.axis_index("row")
    c = lax.axis_index("col")
    y, xh, k = r // 4, (r // 2) % 2, r % 2
    xo = 1 - xh
    q = y * 2 + xh
    sib = {"row": r + 1 - 2 * k}
    yp = {"row": ((y + 1) % 4) * 4 + xh * 2 + k}
    ym = {"row": ((y + 3) % 4) * 4 + xh * 2 + k}
    y2 = {"row": ((y + 2) % 4) * 4 + xh * 2 + k}
    xp = {"row": y * 4 + xo * 2 + k}
    zat = {d: {"col": (c + d + 8) % 8} for d in (1, -1, 2, -2)}
    far = [{"section": 1 - s, "row": (r + j) % 16} for j in range(16)]

    barrier = pltpu.get_barrier_semaphore()
    partners = [sib, yp, ym, y2, xp, {"section": 1 - s}] + list(zat.values())
    for d in partners:
        pl.semaphore_signal(barrier, inc=1, device_id=d, device_id_type=MESH)

    mine = pl.multiple_of(k * H, 128)
    other = pl.multiple_of((1 - k) * H, 128)
    loads = []

    def load(src, dst):
        cp = pltpu.make_async_copy(src, dst, wsem.at[len(loads)])
        cp.start()
        loads.append(cp)

    def load_early():
        load(wg.at[:, pl.ds(mine, H)], WgH.at[0])
        load(wu.at[:, pl.ds(mine, H)], WuH.at[0])

    def load_down():
        load(wd.at[pl.ds(mine, H), :], WdH.at[0])
        send(wd.at[pl.ds(other, H), :], WdX, wx_s.at[2], wx_r.at[2], sib)

    def load_late():
        load(wg.at[:, pl.ds(other, H)], WgH.at[1])
        load(wu.at[:, pl.ds(other, H)], WuH.at[1])
        load(wd.at[pl.ds(other, H), :], WdH.at[1])

    def rows(block):
        return pl.ds(pl.multiple_of(lax.rem(block + 16, 8) * B, 16), B)

    sent = []

    def send(src, dst, ssem, rsem, to):
        cp = pltpu.make_async_remote_copy(
            src_ref=src, dst_ref=dst, send_sem=ssem, recv_sem=rsem, device_id=to, device_id_type=MESH
        )
        cp.start()
        sent.append(cp)
        return cp

    def got(ref, ssem, rsem):
        pltpu.make_async_remote_copy(
            src_ref=ref, dst_ref=ref, send_sem=ssem, recv_sem=rsem, device_id=sib, device_id_type=MESH
        ).wait_recv()

    xs = (x_old, x_cot, x_new)
    kept = []
    for a in range(3):
        cp = pltpu.make_async_copy(xs[a], G.at[a, 0, rows(c), :], xsem.at[a])
        cp.start()
        kept.append(cp)
    load_early()
    pl.semaphore_wait(barrier, len(partners))

    def z_send(a, src, block, j, to):
        ref = G.at[a, 0, rows(block), :]
        send(ref if src is None else src, ref, z_s.at[a, j], z_r.at[a, j], zat[to])

    def z_got(a, block, j):
        ref = G.at[a, 0, rows(block), :]
        got(ref, z_s.at[a, j], z_r.at[a, j])
        send(ref, G.at[a, 1, rows(block), :], gs_s.at[a, j], gs_r.at[a, j], sib)

    def z1(a):
        z_send(a, xs[a], c, 2, 2)
        z_send(a, xs[a], c, 3, -2)
        z_send(a, xs[a], c, 0, 1)
        z_send(a, xs[a], c, 1, -1)
        send(xs[a], G.at[a, 1, rows(c), :], gs_s.at[a, 7], gs_r.at[a, 7], sib)

    def z_near(a):
        z_got(a, c - 1, 0)
        z_got(a, c + 1, 1)

    def z2(a):
        z_got(a, c - 2, 2)
        if a % 2 == 0:
            z_send(a, None, c - 2, 6, 2)
        z_send(a, None, c - 2, 4, 1)
        z_got(a, c + 2, 3)
        if a % 2 == 1:
            z_send(a, None, c + 2, 6, -2)
        z_send(a, None, c + 2, 5, -1)

    def z3(a):
        z_got(a, c - 3, 4)
        z_got(a, c + 3, 5)
        z_got(a, c + 4, 6)

    def z_shared(a):
        kept[a].wait()
        for j in range(8):
            got(G.at[a, 1, rows(c), :], gs_s.at[a, j], gs_r.at[a, j])

    def stage1(a):
        if a == 2:
            def tile(cols):
                acc = dot_nt(G[1, 0], WdH[0, cols, :]) + dot_nt(G[1, 1], WdX[cols, :])
                PS[a, :, cols] = acc.astype(BF)
        else:
            own, theirs = ((WgH, WgX), (WuH, WuX))[a % 3]
            t = 0 if a < 2 else 2

            def tile(cols):
                acc = dot(G[t, 0], own[0, :, cols]) + dot(G[t, 1], theirs[:, cols])
                PS[a, :, cols] = acc.astype(BF)

        tiles(H, 256, tile)
        up, down, across = 2 * (y + 1), 2 * (y - 1), 2 * (y + 2)
        if a in SUM_X:
            for j, block in enumerate((across, up, down, 2 * y)):
                send(PS.at[a, rows(block + xo), :], XQ.at[SUM_X[a], j], rs_s.at[a, j], rs_r.at[a, j], xp)
            return
        send(PS.at[a, rows(across), :], RL.at[a, 0], rs_s.at[a, 0], rs_r.at[a, 0], yp)
        send(PS.at[a, rows(across + 1), :], RL.at[a, 1], rs_s.at[a, 1], rs_r.at[a, 1], ym)
        send(PS.at[a, rows(up + 1), :], PL.at[a, 1], rs_s.at[a, 2], rs_r.at[a, 2], yp)
        send(PS.at[a, rows(down), :], PL.at[a, 0], rs_s.at[a, 3], rs_r.at[a, 3], ym)

    def crossed(a, j, block):
        return PS[a, rows(block + xh), :].astype(F32) + XQ[SUM_X[a], j].astype(F32)

    def stage2x(a):
        n = SUM_X[a]
        got(XQ.at[n, 0], rs_s.at[a, 0], rs_r.at[a, 0])
        SX[n, 0] = crossed(a, 0, 2 * (y + 2)).astype(BF)
        send(SX.at[n, 0, :, LOW], RL.at[a, 0, :, LOW], rs_s.at[a, 4], rs_r.at[a, 4], yp)
        send(SX.at[n, 0, :, HIGH], RL.at[a, 0, :, HIGH], rs_s.at[a, 5], rs_r.at[a, 5], ym)
        got(XQ.at[n, 1], rs_s.at[a, 1], rs_r.at[a, 1])
        SX[n, 1] = crossed(a, 1, 2 * (y + 1)).astype(BF)
        send(SX.at[n, 1, :, HIGH], PL.at[a, 0, :, HIGH], rs_s.at[a, 6], rs_r.at[a, 6], yp)
        got(XQ.at[n, 2], rs_s.at[a, 2], rs_r.at[a, 2])
        SX[n, 2] = crossed(a, 2, 2 * (y - 1)).astype(BF)
        send(SX.at[n, 2, :, LOW], PL.at[a, 0, :, LOW], rs_s.at[a, 7], rs_r.at[a, 7], ym)
        got(XQ.at[n, 3], rs_s.at[a, 3], rs_r.at[a, 3])
        KS[a] = crossed(a, 3, 2 * y)

    def stage3x(a):
        n = SUM_X[a]
        got(RL.at[a, 0, :, LOW], rs_s.at[a, 4], rs_r.at[a, 4])
        full = PS[a, rows(2 * (y + 1) + xh), LOW].astype(F32) + XQ[n, 1, :, LOW].astype(F32)
        AD[a, 0, :, LOW] = (full + RL[a, 0, :, LOW].astype(F32)).astype(BF)
        send(AD.at[a, 0, :, LOW], AR.at[a, 0, :, LOW], rs_s.at[a, 8], rs_r.at[a, 8], yp)
        got(RL.at[a, 0, :, HIGH], rs_s.at[a, 5], rs_r.at[a, 5])
        full = PS[a, rows(2 * (y - 1) + xh), HIGH].astype(F32) + XQ[n, 2, :, HIGH].astype(F32)
        AD[a, 0, :, HIGH] = (full + RL[a, 0, :, HIGH].astype(F32)).astype(BF)
        send(AD.at[a, 0, :, HIGH], AR.at[a, 0, :, HIGH], rs_s.at[a, 9], rs_r.at[a, 9], ym)

    def stage4x(a):
        for j, cols in ((6, HIGH), (7, LOW), (8, LOW), (9, HIGH)):
            got(RL.at[a, 0, :, cols], rs_s.at[a, j], rs_r.at[a, j])

    def stage2(a):
        up, down = 2 * (y + 1), 2 * (y - 1)
        got(RL.at[a, 0], rs_s.at[a, 0], rs_r.at[a, 0])
        AD[a, 0] = (PS[a, rows(up), :].astype(F32) + RL[a, 0].astype(F32)).astype(BF)
        send(AD.at[a, 0], AR.at[a, 0], rs_s.at[a, 4], rs_r.at[a, 4], yp)
        got(RL.at[a, 1], rs_s.at[a, 1], rs_r.at[a, 1])
        AD[a, 1] = (PS[a, rows(down + 1), :].astype(F32) + RL[a, 1].astype(F32)).astype(BF)
        send(AD.at[a, 1], AR.at[a, 1], rs_s.at[a, 5], rs_r.at[a, 5], ym)

    def stage3(a):
        got(PL.at[a, 1], rs_s.at[a, 2], rs_r.at[a, 2])
        got(PL.at[a, 0], rs_s.at[a, 3], rs_r.at[a, 3])
        got(AR.at[a, 0], rs_s.at[a, 4], rs_r.at[a, 4])
        got(AR.at[a, 1], rs_s.at[a, 5], rs_r.at[a, 5])

        def total(which):
            return (
                PS[a, rows(2 * y + which), :].astype(F32)
                + PL[a, which].astype(F32)
                + AR[a, which].astype(F32)
            )

        XS[a] = total(xo).astype(BF)
        send(XS.at[a], XR.at[a], rs_s.at[a, 6], rs_r.at[a, 6], xp)
        KS[a] = total(xh)

    def stage4(a):
        got(XR.at[a], rs_s.at[a, 6], rs_r.at[a, 6])

    def value(a, cols):
        if a in SUM_X:
            return KS[a, :, cols] + PL[a, 0, :, cols].astype(F32) + AR[a, 0, :, cols].astype(F32)
        return KS[a, :, cols] + XR[a, :, cols].astype(F32)

    def sigmoid(v):
        return 1.0 / (1.0 + jnp.exp(-v))

    def activate_new():
        def tile(cols):
            gate, up = value(3, cols), value(4, cols)
            A[0, 0, rows(q), cols] = (gate * sigmoid(gate) * up).astype(BF)

        tiles(H, 128, tile)

    def activate_old():
        def tile(cols):
            gate, up, d = value(0, cols), value(1, cols), value(2, cols)
            sg = sigmoid(gate)
            A[1, 0, rows(q), cols] = (d * up * sg * (1.0 + gate * (1.0 - sg))).astype(BF)
            A[2, 0, rows(q), cols] = (d * gate * sg).astype(BF)
            A[3, 0, rows(q), cols] = (gate * sg * up).astype(BF)

        tiles(H, 128, tile)

    def share(b, ref, block, j):
        send(ref, A.at[b, 1, rows(block), :], cs_s.at[b, j], cs_r.at[b, j], sib)

    def c1(b):
        ref = A.at[b, 0, rows(q), :]
        send(ref, ref, cx_s.at[b, 0], cx_r.at[b, 0], xp)
        send(ref, ref, cy_s.at[b, 0, xh], cy_r.at[b, 0, xh], yp)
        send(ref, ref, cy_s.at[b, 1, xh], cy_r.at[b, 1, xh], ym)
        share(b, ref, q, 0)

    def c2(b):
        block = 2 * y + xo
        ref = A.at[b, 0, rows(block), :]
        got(ref, cx_s.at[b, 0], cx_r.at[b, 0])
        send(ref, ref, cy_s.at[b, 0, xo], cy_r.at[b, 0, xo], yp)
        send(ref, ref, cy_s.at[b, 1, xo], cy_r.at[b, 1, xo], ym)
        share(b, ref, block, 1)

    def c3(b):
        block = 2 * (y - 1)
        ref = A.at[b, 0, rows(block), :]
        got(ref, cy_s.at[b, 0, 0], cy_r.at[b, 0, 0])
        send(ref, ref, cr_s.at[b, 0], cr_r.at[b, 0], yp)
        share(b, ref, block, 2)
        block = 2 * (y + 1) + 1
        ref = A.at[b, 0, rows(block), :]
        got(ref, cy_s.at[b, 1, 1], cy_r.at[b, 1, 1])
        send(ref, ref, cr_s.at[b, 1], cr_r.at[b, 1], ym)
        share(b, ref, block, 3)

    def c4(b):
        for j, (block, sem_s, sem_r) in enumerate((
            (2 * (y - 1) + 1, cy_s.at[b, 0, 1], cy_r.at[b, 0, 1]),
            (2 * (y + 1), cy_s.at[b, 1, 0], cy_r.at[b, 1, 0]),
            (2 * (y + 2), cr_s.at[b, 0], cr_r.at[b, 0]),
            (2 * (y + 2) + 1, cr_s.at[b, 1], cr_r.at[b, 1]),
        )):
            ref = A.at[b, 0, rows(block), :]
            got(ref, sem_s, sem_r)
            share(b, ref, block, 4 + j)

    def direct(b, block, which):
        ref = A.at[b, 0, rows(block), :]
        send(ref, ref, cr_s.at[b, which], cr_r.at[b, which], y2)

    def c3d(b):
        for j, (block, side, which) in enumerate(((2 * (y - 1), 0, 0), (2 * (y + 1) + 1, 1, 1))):
            ref = A.at[b, 0, rows(block), :]
            got(ref, cy_s.at[b, side, which], cy_r.at[b, side, which])
            share(b, ref, block, 2 + j)

    def c1x(b):
        ref = A.at[b, 0, rows(q), :]
        send(ref, ref, cy_s.at[b, 0, 0], cy_r.at[b, 0, 0], yp)
        send(ref, ref, cy_s.at[b, 1, 0], cy_r.at[b, 1, 0], ym)
        send(ref, ref, cx_s.at[b, 0], cx_r.at[b, 0], xp)
        share(b, ref, q, 0)

    def c2x(b):
        for side, sign, cols, to in ((0, -1, LOW, yp), (1, 1, HIGH, ym)):
            block = 2 * (y + sign) + xh
            ref = A.at[b, 0, rows(block), :]
            got(ref, cy_s.at[b, side, 0], cy_r.at[b, side, 0])
            part = A.at[b, 0, rows(block), cols]
            send(part, part, cr_s.at[b, side], cr_r.at[b, side], to)
            send(ref, ref, cx_s.at[b, 1 + side], cx_r.at[b, 1 + side], xp)
            share(b, ref, block, 1 + side)

    def c3x(b):
        block = 2 * (y + 2) + xh
        ref = A.at[b, 0, rows(block), :]
        got(A.at[b, 0, rows(block), LOW], cr_s.at[b, 0], cr_r.at[b, 0])
        got(A.at[b, 0, rows(block), HIGH], cr_s.at[b, 1], cr_r.at[b, 1])
        send(ref, ref, cx_s.at[b, 3], cx_r.at[b, 3], xp)
        share(b, ref, block, 3)

    def c4x(b):
        for j, place in enumerate((y, y - 1, y + 1, y + 2)):
            ref = A.at[b, 0, rows(2 * place + xo), :]
            got(ref, cx_s.at[b, j], cx_r.at[b, j])
            share(b, ref, 2 * place + xo, 4 + j)

    def c5(b):
        for j in range(8):
            got(A.at[b, 1, rows(q), :], cs_s.at[b, j], cs_r.at[b, j])

    def part_out():
        def tile(cols):
            acc = dot(A[0, 0], WdH[0, :, cols]) + dot(A[0, 1], WdH[1, :, cols])
            TT[0, :, cols] = acc.astype(BF)

        tiles(DW, 256, tile)

    def part_gate():
        def tile(cols):
            AC[:, cols] = dot_nt(A[1, 0], WgH[0, cols, :]) + dot_nt(A[1, 1], WgH[1, cols, :])

        tiles(DW, 256, tile)

    def part_grad():
        def tile(cols):
            acc = dot_nt(A[2, 0], WuH[0, cols, :]) + dot_nt(A[2, 1], WuH[1, cols, :])
            TT[1, :, cols] = (AC[:, cols] + acc).astype(BF)

        tiles(DW, 256, tile)

    def z_order(e):
        def tile(cols):
            OP[e, :, cols] = dot(PM[...], TT[e, :, cols]).astype(BF)

        tiles(DW, 256, tile)

    def d1(e):
        def out(block, side, j, to):
            send(OP.at[e, rows(block), :], RD.at[e, side, j], d_s.at[e, side, j], d_r.at[e, side, j], zat[to])

        far_side = e % 2
        sign = 1 if far_side == 0 else -1
        out(c + 4, far_side, 3, 2 * sign)
        out(c + 3, 0, 2, 1)
        out(c - 3, 1, 2, -1)
        out(c + 1, 0, 0, 1)
        out(c - 1, 1, 0, -1)

    def d_got(e, side, j):
        got(RD.at[e, side, j], d_s.at[e, side, j], d_r.at[e, side, j])
        return RD[e, side, j].astype(F32)

    def d2(e):
        for side, sign in ((0, 1), (1, -1)):
            acc = OP[e, rows(c + 2 * sign), :].astype(F32) + d_got(e, side, 2)
            if side == e % 2:
                acc += d_got(e, side, 3)
            ZS[e, side] = acc.astype(BF)
            send(ZS.at[e, side], RD.at[e, side, 1], d_s.at[e, side, 1], d_r.at[e, side, 1], zat[2 * sign])

    def residual(e):
        RES[e] = dot(PM[rows(c), :], G[2 if e == 0 else 1, 0])

    def d_last(e):
        full = OP[e, rows(c), :].astype(F32)
        full += d_got(e, 0, 0) + d_got(e, 1, 0) + d_got(e, 0, 1) + d_got(e, 1, 1)
        full = (full + RES[e]).astype(BF)
        for j in range(4):
            LS[e, j * B : (j + 1) * B, :] = full[:, j * 128 : (j + 1) * 128]

    def e_send(e):
        ES[e] = dot(SP[...], LS[e]).astype(BF)
        for j in range(16):
            there = pl.ds(pl.multiple_of(((r + j) % 16) * 16, 16), 16)
            here = pl.ds(pl.multiple_of(r * 16, 16), 16)
            send(ES.at[e, there, :], ED.at[e, here, :], e_s.at[e, j], e_r.at[e, j], far[j])

    def e_wait(e):
        for j in range(16):
            got(ED.at[e, pl.ds(0, 16), :], e_s.at[e, j], e_r.at[e, j])

    outs = []

    def put(src, dst):
        cp = pltpu.make_async_copy(src, dst, osem.at[len(outs)])
        cp.start()
        outs.append(cp)

    def grad_in(b, h):
        def tile(cols):
            GG[b - 1, h, :, cols] = dot(ST[...], A[b, h, :, cols]).astype(BF)

        tiles(H, 256, tile)
        put(GG.at[b - 1, h], (o_gg, o_gu)[b - 1].at[:, pl.ds((mine, other)[h], H)])

    def grad_out(h):
        def tile(cols):
            GD[h, cols, :] = lax.dot_general(
                A[3, h, :, cols], G[1, 0], (((0,), (0,)), ((), ())), preferred_element_type=F32
            ).astype(BF)

        tiles(H, 256, tile)
        put(GD.at[h], o_gd.at[pl.ds((mine, other)[h], H), :])

    z1(0)
    send(wu.at[:, pl.ds(other, H)], WuX, wx_s.at[1], wx_r.at[1], sib)
    send(wg.at[:, pl.ds(other, H)], WgX, wx_s.at[0], wx_r.at[0], sib)

    pi = lax.broadcasted_iota(jnp.int32, (T, T), 0)
    ti = lax.broadcasted_iota(jnp.int32, (T, T), 1)
    token = ((pi % B) // 3) * 24 + (pi // B) * 3 + pi % 3
    PM[...] = jnp.where(ti == token, 1.0, 0.0).astype(BF)

    z_near(0)
    z2(0)
    z1(1)

    ri = lax.broadcasted_iota(jnp.int32, (256, 4 * B), 0)
    li = lax.broadcasted_iota(jnp.int32, (256, 4 * B), 1)
    sub = ri % 16
    hit = (sub < 12) & (li // B == sub // 3) & (li % B == (ri // 16) * 3 + sub % 3)
    SP[...] = jnp.where(hit, 1.0, 0.0).astype(BF)

    z3(0)
    load_down()
    z_near(1)
    z2(1)
    z1(2)
    loads[1].wait()
    got(WuX, wx_s.at[1], wx_r.at[1])
    z_shared(0)
    stage1(1)
    loads[0].wait()
    got(WgX, wx_s.at[0], wx_r.at[0])
    stage1(0)
    z_near(2)
    z2(2)
    z3(1)
    loads[2].wait()
    got(WdX, wx_s.at[2], wx_r.at[2])
    z_shared(1)
    stage1(2)
    load_late()
    stage2(0)
    z3(2)
    stage2x(1)
    ST[...] = jnp.transpose(G[0, 0])
    residual(1)
    z_shared(2)
    stage1(3)
    stage1(4)
    residual(0)
    stage2(2)
    stage3(0)
    stage3x(1)
    stage2x(3)
    stage2(4)
    stage3(2)
    stage4(0)
    stage4x(1)
    stage4(2)
    activate_old()
    c1x(2)
    c1(1)
    stage3x(3)
    stage3(4)
    c2x(2)
    c2(1)
    c3x(2)
    c3(1)
    stage4x(3)
    stage4(4)
    activate_new()
    c1(0)
    direct(0, q, xh)
    c4(1)
    c2(0)
    direct(0, 2 * y + xo, xo)
    c4x(2)
    for cp in loads[3:]:
        cp.wait()
    c5(1)
    pl.semaphore_signal(row_sem, inc=1, device_id={"section": 1 - s}, device_id_type=MESH)
    part_gate()
    c5(2)
    part_grad()
    z_order(1)
    d1(1)
    c3d(0)
    c4(0)
    c1(3)
    c5(0)
    part_out()
    z_order(0)
    d1(0)
    d2(1)
    c2(3)
    d2(0)
    c3(3)
    d_last(1)
    pl.semaphore_wait(row_sem, 1)
    e_send(1)
    grad_in(1, 0)
    c4(3)
    d_last(0)
    e_send(0)
    grad_in(1, 1)
    grad_in(2, 0)
    grad_in(2, 1)
    c5(3)
    grad_out(0)
    grad_out(1)
    e_wait(0)
    e_wait(1)
    o_seen[...] = ED[...]
    for cp in outs:
        cp.wait()
    for cp in sent:
        cp.wait_send()


def finish(seen, gg, gu, gd, o_next, o_grad, o_gg, o_gu, o_gd, sem):
    copies = []
    for i, (src, dst) in enumerate(((gg, o_gg), (gu, o_gu), (gd, o_gd))):
        part = src.shape[0] // 4
        for j in range(4):
            here = pl.ds(j * part, part)
            cp = pltpu.make_async_copy(src.at[here, :], dst.at[0, here, :], sem.at[i, j])
            cp.start()
            copies.append(cp)
    for e, dst in enumerate((o_next, o_grad)):
        for j in range(16):
            for i in range(4):
                at = j * DW + i * 128
                dst[0, :, at : at + 128] = seen[e, j * 16 + i * 3 : j * 16 + i * 3 + 3, :]
    for cp in copies:
        cp.wait()


def body(fwd_in, bwd_in, cotangent, w_gate, w_up, w_down):
    vmem = pl.BlockSpec(memory_space=pltpu.VMEM)
    hbm = pl.BlockSpec(memory_space=pltpu.HBM)
    V = pltpu.VMEM
    D = pltpu.SemaphoreType.DMA
    scratch = [
        V((3, 2, T, DW), BF),
        V((2, DW, H), BF), V((2, DW, H), BF), V((2, H, DW), BF),
        V((DW, H), BF), V((DW, H), BF), V((H, DW), BF),
        V((5, T, H), BF),
        V((5, 2, B, H), BF), V((5, 2, B, H), BF), V((5, 2, B, H), BF), V((5, 2, B, H), BF),
        V((5, B, H), F32), V((5, B, H), BF), V((5, B, H), BF),
        V((2, 4, B, H), BF), V((2, 3, B, H), BF),
        V((4, 2, T, H), BF),
        V((2, T, DW), BF), V((T, DW), F32), V((2, T, DW), BF),
        V((2, 2, B, DW), BF), V((2, 2, 4, B, DW), BF),
        V((2, B, DW), F32), V((2, 4 * B, 128), BF), V((2, 256, 128), BF), V((2, 256, 128), BF),
        V((T, T), BF), V((256, 4 * B), BF), V((DW, T), BF),
        V((2, 2, DW, H), BF), V((2, H, DW), BF),
        D((6,)), D((3,)), D((3, 7)), D((3, 7)), D((3, 8)), D((3, 8)), D((3,)), D((3,)),
        D((5, 10)), D((5, 10)), D((4, 2, 2)), D((4, 2, 2)), D((4, 2)), D((4, 2)),
        D((4, 4)), D((4, 4)), D((4, 8)), D((4, 8)),
        D((2, 2, 4)), D((2, 2, 4)), D((2, 16)), D((2, 16)), D((6,)), pltpu.SemaphoreType.REGULAR,
    ]
    seen, gg, gu, gd = pl.pallas_call(
        kernel,
        out_shape=(
            jax.ShapeDtypeStruct((2, 256, 128), BF),
            jax.ShapeDtypeStruct((DW, 2 * H), BF),
            jax.ShapeDtypeStruct((DW, 2 * H), BF),
            jax.ShapeDtypeStruct((2 * H, DW), BF),
        ),
        in_specs=[vmem] * 3 + [hbm] * 3,
        out_specs=(vmem, hbm, hbm, hbm),
        scratch_shapes=scratch,
        compiler_params=pltpu.CompilerParams(
            collective_id=0, has_side_effects=True, vmem_limit_bytes=48 * 2**20
        ),
        cost_estimate=pl.CostEstimate(flops=8 * 10**9, bytes_accessed=12 * 10**6, transcendentals=0),
        name="relay",
    )(fwd_in[0], bwd_in[0], cotangent[0], w_gate[0], w_up[0], w_down[0])
    return pl.pallas_call(
        finish,
        out_shape=(
            jax.ShapeDtypeStruct((1, 3, 16 * DW), BF),
            jax.ShapeDtypeStruct((1, 3, 16 * DW), BF),
            jax.ShapeDtypeStruct((1, DW, 2 * H), BF),
            jax.ShapeDtypeStruct((1, DW, 2 * H), BF),
            jax.ShapeDtypeStruct((1, 2 * H, DW), BF),
        ),
        in_specs=[vmem, hbm, hbm, hbm],
        out_specs=(vmem, vmem, hbm, hbm, hbm),
        scratch_shapes=[pltpu.SemaphoreType.DMA((3, 4))],
        compiler_params=pltpu.CompilerParams(vmem_limit_bytes=16 * 2**20),
        name="finish",
    )(seen, gg, gu, gd)


def solution(mesh):
    in_specs = (
        P("section", "col", "row"),
        P("section", "col", "row"),
        P("section", "col", "row"),
        P("section", "row", "col"),
        P("section", "row", "col"),
        P("section", "col", "row"),
    )
    out_specs = (
        P("section", ("row", "col"), None),
        P("section", ("row", "col"), None),
        P("section", "row", "col"),
        P("section", "row", "col"),
        P("section", "col", "row"),
    )
    return jax.shard_map(body, mesh=mesh, in_specs=in_specs, out_specs=out_specs, check_vma=False)
```

```python
import functools

import jax
import jax.numpy as jnp
from jax import lax
from jax.experimental import pallas as pl
from jax.experimental.pallas import tpu as pltpu
from jax.sharding import PartitionSpec as P

MESH = pl.DeviceIdType.MESH
BF = jnp.bfloat16
F32 = jnp.float32
T = 384
B = 48
DW = 512
H = 896
LOW, HIGH = pl.ds(0, 512), pl.ds(512, 384)
SUM_X = {1: 0, 3: 1}


def dot(left, right):
    return lax.dot_general(left, right, (((1,), (0,)), ((), ())), preferred_element_type=F32)


def dot_nt(left, right):
    return lax.dot_general(left, right, (((1,), (1,)), ((), ())), preferred_element_type=F32)


def tiles(width, step, body):
    whole = width // step

    @pl.loop(0, whole)
    def _(i):
        body(pl.ds(pl.multiple_of(i * step, step), step))

    if width % step:
        body(pl.ds(whole * step, width % step))


def kernel(
    x_new, x_old, x_cot, wg, wu, wd,
    o_seen, o_gg, o_gu, o_gd,
    G, WgH, WuH, WdH, WgX, WuX, WdX,
    PS, RL, PL, AD, AR, KS, XS, XR, XQ, SX,
    A, TT, AC, OP, ZS, RD, RES, LS, ES, ED, PM, SP, ST, GG, GD,
    wsem, xsem, z_s, z_r, gs_s, gs_r, wx_s, wx_r,
    rs_s, rs_r, cy_s, cy_r, cr_s, cr_r, cx_s, cx_r, cs_s, cs_r,
    d_s, d_r, e_s, e_r, osem, row_sem,
):
    s = lax.axis_index("section")
    r = lax.axis_index("row")
    c = lax.axis_index("col")
    y, xh, k = r // 4, (r // 2) % 2, r % 2
    xo = 1 - xh
    q = y * 2 + xh
    sib = {"row": r + 1 - 2 * k}
    yp = {"row": ((y + 1) % 4) * 4 + xh * 2 + k}
    ym = {"row": ((y + 3) % 4) * 4 + xh * 2 + k}
    y2 = {"row": ((y + 2) % 4) * 4 + xh * 2 + k}
    xp = {"row": y * 4 + xo * 2 + k}
    zat = {d: {"col": (c + d + 8) % 8} for d in (1, -1, 2, -2)}
    far = [{"section": 1 - s, "row": (r + j) % 16} for j in range(16)]

    barrier = pltpu.get_barrier_semaphore()
    partners = [sib, yp, ym, y2, xp, {"section": 1 - s}] + list(zat.values())
    for d in partners:
        pl.semaphore_signal(barrier, inc=1, device_id=d, device_id_type=MESH)

    mine = pl.multiple_of(k * H, 128)
    other = pl.multiple_of((1 - k) * H, 128)
    loads = []

    def load(src, dst):
        cp = pltpu.make_async_copy(src, dst, wsem.at[len(loads)])
        cp.start()
        loads.append(cp)

    def load_early():
        load(wg.at[:, pl.ds(mine, H)], WgH.at[0])
        load(wu.at[:, pl.ds(mine, H)], WuH.at[0])

    def load_down():
        load(wd.at[pl.ds(mine, H), :], WdH.at[0])
        send(wd.at[pl.ds(other, H), :], WdX, wx_s.at[2], wx_r.at[2], sib)

    def load_late():
        load(wg.at[:, pl.ds(other, H)], WgH.at[1])
        load(wu.at[:, pl.ds(other, H)], WuH.at[1])
        load(wd.at[pl.ds(other, H), :], WdH.at[1])

    def rows(block):
        return pl.ds(pl.multiple_of(lax.rem(block + 16, 8) * B, 16), B)

    sent = []

    def send(src, dst, ssem, rsem, to):
        cp = pltpu.make_async_remote_copy(
            src_ref=src, dst_ref=dst, send_sem=ssem, recv_sem=rsem, device_id=to, device_id_type=MESH
        )
        cp.start()
        sent.append(cp)
        return cp

    def got(ref, ssem, rsem):
        pltpu.make_async_remote_copy(
            src_ref=ref, dst_ref=ref, send_sem=ssem, recv_sem=rsem, device_id=sib, device_id_type=MESH
        ).wait_recv()

    xs = (x_old, x_cot, x_new)
    kept = []
    for a in range(3):
        cp = pltpu.make_async_copy(xs[a], G.at[a, 0, rows(c), :], xsem.at[a])
        cp.start()
        kept.append(cp)
    load_early()
    pl.semaphore_wait(barrier, len(partners))

    def z_send(a, src, block, j, to):
        ref = G.at[a, 0, rows(block), :]
        send(ref if src is None else src, ref, z_s.at[a, j], z_r.at[a, j], zat[to])

    def z_got(a, block, j):
        ref = G.at[a, 0, rows(block), :]
        got(ref, z_s.at[a, j], z_r.at[a, j])
        send(ref, G.at[a, 1, rows(block), :], gs_s.at[a, j], gs_r.at[a, j], sib)

    def z1(a):
        z_send(a, xs[a], c, 2, 2)
        z_send(a, xs[a], c, 3, -2)
        z_send(a, xs[a], c, 0, 1)
        z_send(a, xs[a], c, 1, -1)
        send(xs[a], G.at[a, 1, rows(c), :], gs_s.at[a, 7], gs_r.at[a, 7], sib)

    def z_near(a):
        z_got(a, c - 1, 0)
        z_got(a, c + 1, 1)

    def z2(a):
        z_got(a, c - 2, 2)
        if a % 2 == 0:
            z_send(a, None, c - 2, 6, 2)
        z_send(a, None, c - 2, 4, 1)
        z_got(a, c + 2, 3)
        if a % 2 == 1:
            z_send(a, None, c + 2, 6, -2)
        z_send(a, None, c + 2, 5, -1)

    def z3(a):
        z_got(a, c - 3, 4)
        z_got(a, c + 3, 5)
        z_got(a, c + 4, 6)

    def z_shared(a):
        kept[a].wait()
        for j in range(8):
            got(G.at[a, 1, rows(c), :], gs_s.at[a, j], gs_r.at[a, j])

    def stage1(a):
        if a == 2:
            def tile(cols):
                acc = dot_nt(G[1, 0], WdH[0, cols, :]) + dot_nt(G[1, 1], WdX[cols, :])
                PS[a, :, cols] = acc.astype(BF)
        else:
            own, theirs = ((WgH, WgX), (WuH, WuX))[a % 3]
            t = 0 if a < 2 else 2

            def tile(cols):
                acc = dot(G[t, 0], own[0, :, cols]) + dot(G[t, 1], theirs[:, cols])
                PS[a, :, cols] = acc.astype(BF)

        tiles(H, 256, tile)
        up, down, across = 2 * (y + 1), 2 * (y - 1), 2 * (y + 2)
        if a in SUM_X:
            for j, block in enumerate((across, up, down, 2 * y)):
                send(PS.at[a, rows(block + xo), :], XQ.at[SUM_X[a], j], rs_s.at[a, j], rs_r.at[a, j], xp)
            return
        send(PS.at[a, rows(across), :], RL.at[a, 0], rs_s.at[a, 0], rs_r.at[a, 0], yp)
        send(PS.at[a, rows(across + 1), :], RL.at[a, 1], rs_s.at[a, 1], rs_r.at[a, 1], ym)
        send(PS.at[a, rows(up + 1), :], PL.at[a, 1], rs_s.at[a, 2], rs_r.at[a, 2], yp)
        send(PS.at[a, rows(down), :], PL.at[a, 0], rs_s.at[a, 3], rs_r.at[a, 3], ym)

    def crossed(a, j, block):
        return PS[a, rows(block + xh), :].astype(F32) + XQ[SUM_X[a], j].astype(F32)

    def stage2x(a):
        n = SUM_X[a]
        got(XQ.at[n, 0], rs_s.at[a, 0], rs_r.at[a, 0])
        SX[n, 0] = crossed(a, 0, 2 * (y + 2)).astype(BF)
        send(SX.at[n, 0, :, LOW], RL.at[a, 0, :, LOW], rs_s.at[a, 4], rs_r.at[a, 4], yp)
        send(SX.at[n, 0, :, HIGH], RL.at[a, 0, :, HIGH], rs_s.at[a, 5], rs_r.at[a, 5], ym)
        got(XQ.at[n, 1], rs_s.at[a, 1], rs_r.at[a, 1])
        SX[n, 1] = crossed(a, 1, 2 * (y + 1)).astype(BF)
        send(SX.at[n, 1, :, HIGH], PL.at[a, 0, :, HIGH], rs_s.at[a, 6], rs_r.at[a, 6], yp)
        got(XQ.at[n, 2], rs_s.at[a, 2], rs_r.at[a, 2])
        SX[n, 2] = crossed(a, 2, 2 * (y - 1)).astype(BF)
        send(SX.at[n, 2, :, LOW], PL.at[a, 0, :, LOW], rs_s.at[a, 7], rs_r.at[a, 7], ym)
        got(XQ.at[n, 3], rs_s.at[a, 3], rs_r.at[a, 3])
        KS[a] = crossed(a, 3, 2 * y)

    def stage3x(a):
        n = SUM_X[a]
        got(RL.at[a, 0, :, LOW], rs_s.at[a, 4], rs_r.at[a, 4])
        full = PS[a, rows(2 * (y + 1) + xh), LOW].astype(F32) + XQ[n, 1, :, LOW].astype(F32)
        AD[a, 0, :, LOW] = (full + RL[a, 0, :, LOW].astype(F32)).astype(BF)
        send(AD.at[a, 0, :, LOW], AR.at[a, 0, :, LOW], rs_s.at[a, 8], rs_r.at[a, 8], yp)
        got(RL.at[a, 0, :, HIGH], rs_s.at[a, 5], rs_r.at[a, 5])
        full = PS[a, rows(2 * (y - 1) + xh), HIGH].astype(F32) + XQ[n, 2, :, HIGH].astype(F32)
        AD[a, 0, :, HIGH] = (full + RL[a, 0, :, HIGH].astype(F32)).astype(BF)
        send(AD.at[a, 0, :, HIGH], AR.at[a, 0, :, HIGH], rs_s.at[a, 9], rs_r.at[a, 9], ym)

    def stage4x(a):
        for j, cols in ((6, HIGH), (7, LOW), (8, LOW), (9, HIGH)):
            got(RL.at[a, 0, :, cols], rs_s.at[a, j], rs_r.at[a, j])

    def stage2(a):
        up, down = 2 * (y + 1), 2 * (y - 1)
        got(RL.at[a, 0], rs_s.at[a, 0], rs_r.at[a, 0])
        AD[a, 0] = (PS[a, rows(up), :].astype(F32) + RL[a, 0].astype(F32)).astype(BF)
        send(AD.at[a, 0], AR.at[a, 0], rs_s.at[a, 4], rs_r.at[a, 4], yp)
        got(RL.at[a, 1], rs_s.at[a, 1], rs_r.at[a, 1])
        AD[a, 1] = (PS[a, rows(down + 1), :].astype(F32) + RL[a, 1].astype(F32)).astype(BF)
        send(AD.at[a, 1], AR.at[a, 1], rs_s.at[a, 5], rs_r.at[a, 5], ym)

    def stage3(a):
        got(PL.at[a, 1], rs_s.at[a, 2], rs_r.at[a, 2])
        got(PL.at[a, 0], rs_s.at[a, 3], rs_r.at[a, 3])
        got(AR.at[a, 0], rs_s.at[a, 4], rs_r.at[a, 4])
        got(AR.at[a, 1], rs_s.at[a, 5], rs_r.at[a, 5])

        def total(which):
            return (
                PS[a, rows(2 * y + which), :].astype(F32)
                + PL[a, which].astype(F32)
                + AR[a, which].astype(F32)
            )

        XS[a] = total(xo).astype(BF)
        send(XS.at[a], XR.at[a], rs_s.at[a, 6], rs_r.at[a, 6], xp)
        KS[a] = total(xh)

    def stage4(a):
        got(XR.at[a], rs_s.at[a, 6], rs_r.at[a, 6])

    def value(a, cols):
        if a in SUM_X:
            return KS[a, :, cols] + PL[a, 0, :, cols].astype(F32) + AR[a, 0, :, cols].astype(F32)
        return KS[a, :, cols] + XR[a, :, cols].astype(F32)

    def sigmoid(v):
        return 1.0 / (1.0 + jnp.exp(-v))

    def activate_new():
        def tile(cols):
            gate, up = value(3, cols), value(4, cols)
            A[0, 0, rows(q), cols] = (gate * sigmoid(gate) * up).astype(BF)

        tiles(H, 128, tile)

    def activate_old():
        def tile(cols):
            gate, up, d = value(0, cols), value(1, cols), value(2, cols)
            sg = sigmoid(gate)
            A[1, 0, rows(q), cols] = (d * up * sg * (1.0 + gate * (1.0 - sg))).astype(BF)
            A[2, 0, rows(q), cols] = (d * gate * sg).astype(BF)
            A[3, 0, rows(q), cols] = (gate * sg * up).astype(BF)

        tiles(H, 128, tile)

    def share(b, ref, block, j):
        send(ref, A.at[b, 1, rows(block), :], cs_s.at[b, j], cs_r.at[b, j], sib)

    def c1(b):
        ref = A.at[b, 0, rows(q), :]
        send(ref, ref, cx_s.at[b, 0], cx_r.at[b, 0], xp)
        send(ref, ref, cy_s.at[b, 0, xh], cy_r.at[b, 0, xh], yp)
        send(ref, ref, cy_s.at[b, 1, xh], cy_r.at[b, 1, xh], ym)
        share(b, ref, q, 0)

    def c2(b):
        block = 2 * y + xo
        ref = A.at[b, 0, rows(block), :]
        got(ref, cx_s.at[b, 0], cx_r.at[b, 0])
        send(ref, ref, cy_s.at[b, 0, xo], cy_r.at[b, 0, xo], yp)
        send(ref, ref, cy_s.at[b, 1, xo], cy_r.at[b, 1, xo], ym)
        share(b, ref, block, 1)

    def c3(b):
        block = 2 * (y - 1)
        ref = A.at[b, 0, rows(block), :]
        got(ref, cy_s.at[b, 0, 0], cy_r.at[b, 0, 0])
        send(ref, ref, cr_s.at[b, 0], cr_r.at[b, 0], yp)
        share(b, ref, block, 2)
        block = 2 * (y + 1) + 1
        ref = A.at[b, 0, rows(block), :]
        got(ref, cy_s.at[b, 1, 1], cy_r.at[b, 1, 1])
        send(ref, ref, cr_s.at[b, 1], cr_r.at[b, 1], ym)
        share(b, ref, block, 3)

    def c4(b):
        for j, (block, sem_s, sem_r) in enumerate((
            (2 * (y - 1) + 1, cy_s.at[b, 0, 1], cy_r.at[b, 0, 1]),
            (2 * (y + 1), cy_s.at[b, 1, 0], cy_r.at[b, 1, 0]),
            (2 * (y + 2), cr_s.at[b, 0], cr_r.at[b, 0]),
            (2 * (y + 2) + 1, cr_s.at[b, 1], cr_r.at[b, 1]),
        )):
            ref = A.at[b, 0, rows(block), :]
            got(ref, sem_s, sem_r)
            share(b, ref, block, 4 + j)

    def direct(b, block, which):
        ref = A.at[b, 0, rows(block), :]
        send(ref, ref, cr_s.at[b, which], cr_r.at[b, which], y2)

    def c3d(b):
        for j, (block, side, which) in enumerate(((2 * (y - 1), 0, 0), (2 * (y + 1) + 1, 1, 1))):
            ref = A.at[b, 0, rows(block), :]
            got(ref, cy_s.at[b, side, which], cy_r.at[b, side, which])
            share(b, ref, block, 2 + j)

    def c1x(b):
        ref = A.at[b, 0, rows(q), :]
        send(ref, ref, cy_s.at[b, 0, 0], cy_r.at[b, 0, 0], yp)
        send(ref, ref, cy_s.at[b, 1, 0], cy_r.at[b, 1, 0], ym)
        send(ref, ref, cx_s.at[b, 0], cx_r.at[b, 0], xp)
        share(b, ref, q, 0)

    def c2x(b):
        for side, sign, cols, to in ((0, -1, LOW, yp), (1, 1, HIGH, ym)):
            block = 2 * (y + sign) + xh
            ref = A.at[b, 0, rows(block), :]
            got(ref, cy_s.at[b, side, 0], cy_r.at[b, side, 0])
            part = A.at[b, 0, rows(block), cols]
            send(part, part, cr_s.at[b, side], cr_r.at[b, side], to)
            send(ref, ref, cx_s.at[b, 1 + side], cx_r.at[b, 1 + side], xp)
            share(b, ref, block, 1 + side)

    def c3x(b):
        block = 2 * (y + 2) + xh
        ref = A.at[b, 0, rows(block), :]
        got(A.at[b, 0, rows(block), LOW], cr_s.at[b, 0], cr_r.at[b, 0])
        got(A.at[b, 0, rows(block), HIGH], cr_s.at[b, 1], cr_r.at[b, 1])
        send(ref, ref, cx_s.at[b, 3], cx_r.at[b, 3], xp)
        share(b, ref, block, 3)

    def c4x(b):
        for j, place in enumerate((y, y - 1, y + 1, y + 2)):
            ref = A.at[b, 0, rows(2 * place + xo), :]
            got(ref, cx_s.at[b, j], cx_r.at[b, j])
            share(b, ref, 2 * place + xo, 4 + j)

    def c5(b):
        for j in range(8):
            got(A.at[b, 1, rows(q), :], cs_s.at[b, j], cs_r.at[b, j])

    def part_out():
        def tile(cols):
            acc = dot(A[0, 0], WdH[0, :, cols]) + dot(A[0, 1], WdH[1, :, cols])
            TT[0, :, cols] = acc.astype(BF)

        tiles(DW, 256, tile)

    def part_gate():
        def tile(cols):
            AC[:, cols] = dot_nt(A[1, 0], WgH[0, cols, :]) + dot_nt(A[1, 1], WgH[1, cols, :])

        tiles(DW, 256, tile)

    def part_grad():
        def tile(cols):
            acc = dot_nt(A[2, 0], WuH[0, cols, :]) + dot_nt(A[2, 1], WuH[1, cols, :])
            TT[1, :, cols] = (AC[:, cols] + acc).astype(BF)

        tiles(DW, 256, tile)

    def z_order(e):
        def tile(cols):
            OP[e, :, cols] = dot(PM[...], TT[e, :, cols]).astype(BF)

        tiles(DW, 256, tile)

    def d1(e):
        def out(block, side, j, to):
            send(OP.at[e, rows(block), :], RD.at[e, side, j], d_s.at[e, side, j], d_r.at[e, side, j], zat[to])

        far_side = e % 2
        sign = 1 if far_side == 0 else -1
        out(c + 4, far_side, 3, 2 * sign)
        out(c + 3, 0, 2, 1)
        out(c - 3, 1, 2, -1)
        out(c + 1, 0, 0, 1)
        out(c - 1, 1, 0, -1)

    def d_got(e, side, j):
        got(RD.at[e, side, j], d_s.at[e, side, j], d_r.at[e, side, j])
        return RD[e, side, j].astype(F32)

    def d2(e):
        for side, sign in ((0, 1), (1, -1)):
            acc = OP[e, rows(c + 2 * sign), :].astype(F32) + d_got(e, side, 2)
            if side == e % 2:
                acc += d_got(e, side, 3)
            ZS[e, side] = acc.astype(BF)
            send(ZS.at[e, side], RD.at[e, side, 1], d_s.at[e, side, 1], d_r.at[e, side, 1], zat[2 * sign])

    def residual(e):
        RES[e] = dot(PM[rows(c), :], G[2 if e == 0 else 1, 0])

    def d_last(e):
        full = OP[e, rows(c), :].astype(F32)
        full += d_got(e, 0, 0) + d_got(e, 1, 0) + d_got(e, 0, 1) + d_got(e, 1, 1)
        full = (full + RES[e]).astype(BF)
        for j in range(4):
            LS[e, j * B : (j + 1) * B, :] = full[:, j * 128 : (j + 1) * 128]

    def e_send(e):
        ES[e] = dot(SP[...], LS[e]).astype(BF)
        for j in range(16):
            there = pl.ds(pl.multiple_of(((r + j) % 16) * 16, 16), 16)
            here = pl.ds(pl.multiple_of(r * 16, 16), 16)
            send(ES.at[e, there, :], ED.at[e, here, :], e_s.at[e, j], e_r.at[e, j], far[j])

    def e_wait(e):
        for j in range(16):
            got(ED.at[e, pl.ds(0, 16), :], e_s.at[e, j], e_r.at[e, j])

    outs = []

    def put(src, dst):
        cp = pltpu.make_async_copy(src, dst, osem.at[len(outs)])
        cp.start()
        outs.append(cp)

    def grad_in(b, h):
        def tile(cols):
            GG[b - 1, h, :, cols] = dot(ST[...], A[b, h, :, cols]).astype(BF)

        tiles(H, 256, tile)
        put(GG.at[b - 1, h], (o_gg, o_gu)[b - 1].at[:, pl.ds((mine, other)[h], H)])

    def grad_out(h):
        def tile(cols):
            GD[h, cols, :] = lax.dot_general(
                A[3, h, :, cols], G[1, 0], (((0,), (0,)), ((), ())), preferred_element_type=F32
            ).astype(BF)

        tiles(H, 256, tile)
        put(GD.at[h], o_gd.at[pl.ds((mine, other)[h], H), :])

    z1(0)
    send(wu.at[:, pl.ds(other, H)], WuX, wx_s.at[1], wx_r.at[1], sib)
    send(wg.at[:, pl.ds(other, H)], WgX, wx_s.at[0], wx_r.at[0], sib)

    pi = lax.broadcasted_iota(jnp.int32, (T, T), 0)
    ti = lax.broadcasted_iota(jnp.int32, (T, T), 1)
    token = ((pi % B) // 3) * 24 + (pi // B) * 3 + pi % 3
    PM[...] = jnp.where(ti == token, 1.0, 0.0).astype(BF)

    z_near(0)
    z2(0)
    z1(1)

    ri = lax.broadcasted_iota(jnp.int32, (256, 4 * B), 0)
    li = lax.broadcasted_iota(jnp.int32, (256, 4 * B), 1)
    sub = ri % 16
    hit = (sub < 12) & (li // B == sub // 3) & (li % B == (ri // 16) * 3 + sub % 3)
    SP[...] = jnp.where(hit, 1.0, 0.0).astype(BF)

    z3(0)
    load_down()
    z_near(1)
    z2(1)
    z1(2)
    loads[1].wait()
    got(WuX, wx_s.at[1], wx_r.at[1])
    z_shared(0)
    stage1(1)
    loads[0].wait()
    got(WgX, wx_s.at[0], wx_r.at[0])
    stage1(0)
    z_near(2)
    z2(2)
    z3(1)
    loads[2].wait()
    got(WdX, wx_s.at[2], wx_r.at[2])
    z_shared(1)
    stage1(2)
    load_late()
    stage2(0)
    z3(2)
    stage2x(1)
    ST[...] = jnp.transpose(G[0, 0])
    residual(1)
    z_shared(2)
    stage1(3)
    stage1(4)
    residual(0)
    stage2(2)
    stage3(0)
    stage3x(1)
    stage2x(3)
    stage2(4)
    stage3(2)
    stage4(0)
    stage4x(1)
    stage4(2)
    activate_old()
    c1x(2)
    c1(1)
    stage3x(3)
    stage3(4)
    c2x(2)
    c2(1)
    c3x(2)
    c3(1)
    stage4x(3)
    stage4(4)
    activate_new()
    c1(0)
    direct(0, q, xh)
    c4(1)
    c2(0)
    direct(0, 2 * y + xo, xo)
    c4x(2)
    for cp in loads[3:]:
        cp.wait()
    c5(1)
    pl.semaphore_signal(row_sem, inc=1, device_id={"section": 1 - s}, device_id_type=MESH)
    part_gate()
    c5(2)
    part_grad()
    z_order(1)
    d1(1)
    c3d(0)
    c4(0)
    c1(3)
    c5(0)
    part_out()
    z_order(0)
    d1(0)
    d2(1)
    c2(3)
    d2(0)
    c3(3)
    d_last(1)
    pl.semaphore_wait(row_sem, 1)
    e_send(1)
    grad_in(1, 0)
    c4(3)
    d_last(0)
    e_send(0)
    grad_in(1, 1)
    grad_in(2, 0)
    grad_in(2, 1)
    c5(3)
    grad_out(0)
    grad_out(1)
    e_wait(0)
    e_wait(1)
    o_seen[...] = ED[...]
    for cp in outs:
        cp.wait()
    for cp in sent:
        cp.wait_send()


def finish(seen, gg, gu, gd, o_next, o_grad, o_gg, o_gu, o_gd, tok, sem, tsem):
    copies = []
    for i, (src, dst) in enumerate(((gg, o_gg), (gu, o_gu), (gd, o_gd))):
        part = src.shape[0] // 4
        for j in range(4):
            here = pl.ds(j * part, part)
            cp = pltpu.make_async_copy(src.at[here, :], dst.at[0, here, :], sem.at[i, j])
            cp.start()
            copies.append(cp)
    for e, dst in enumerate((o_next, o_grad)):
        part = tok.at[e]
        for j in range(16):
            for i in range(4):
                at = j * DW + i * 128
                part[0, :, at : at + 128] = seen[e, j * 16 + i * 3 : j * 16 + i * 3 + 3, :]
        cp = pltpu.make_async_copy(part, dst, tsem.at[e])
        cp.start()
        copies.append(cp)
    for cp in copies:
        cp.wait()


def body(fwd_in, bwd_in, cotangent, w_gate, w_up, w_down):
    vmem = pl.BlockSpec(memory_space=pltpu.VMEM)
    hbm = pl.BlockSpec(memory_space=pltpu.HBM)
    V = pltpu.VMEM
    D = pltpu.SemaphoreType.DMA
    scratch = [
        V((3, 2, T, DW), BF),
        V((2, DW, H), BF), V((2, DW, H), BF), V((2, H, DW), BF),
        V((DW, H), BF), V((DW, H), BF), V((H, DW), BF),
        V((5, T, H), BF),
        V((5, 2, B, H), BF), V((5, 2, B, H), BF), V((5, 2, B, H), BF), V((5, 2, B, H), BF),
        V((5, B, H), F32), V((5, B, H), BF), V((5, B, H), BF),
        V((2, 4, B, H), BF), V((2, 3, B, H), BF),
        V((4, 2, T, H), BF),
        V((2, T, DW), BF), V((T, DW), F32), V((2, T, DW), BF),
        V((2, 2, B, DW), BF), V((2, 2, 4, B, DW), BF),
        V((2, B, DW), F32), V((2, 4 * B, 128), BF), V((2, 256, 128), BF), V((2, 256, 128), BF),
        V((T, T), BF), V((256, 4 * B), BF), V((DW, T), BF),
        V((2, 2, DW, H), BF), V((2, H, DW), BF),
        D((6,)), D((3,)), D((3, 7)), D((3, 7)), D((3, 8)), D((3, 8)), D((3,)), D((3,)),
        D((5, 10)), D((5, 10)), D((4, 2, 2)), D((4, 2, 2)), D((4, 2)), D((4, 2)),
        D((4, 4)), D((4, 4)), D((4, 8)), D((4, 8)),
        D((2, 2, 4)), D((2, 2, 4)), D((2, 16)), D((2, 16)), D((6,)), pltpu.SemaphoreType.REGULAR,
    ]
    seen, gg, gu, gd = pl.pallas_call(
        kernel,
        out_shape=(
            jax.ShapeDtypeStruct((2, 256, 128), BF),
            jax.ShapeDtypeStruct((DW, 2 * H), BF),
            jax.ShapeDtypeStruct((DW, 2 * H), BF),
            jax.ShapeDtypeStruct((2 * H, DW), BF),
        ),
        in_specs=[vmem] * 3 + [hbm] * 3,
        out_specs=(vmem, hbm, hbm, hbm),
        scratch_shapes=scratch,
        compiler_params=pltpu.CompilerParams(
            collective_id=0, has_side_effects=True, vmem_limit_bytes=48 * 2**20
        ),
        cost_estimate=pl.CostEstimate(flops=8 * 10**9, bytes_accessed=12 * 10**6, transcendentals=0),
        name="relay",
    )(fwd_in[0], bwd_in[0], cotangent[0], w_gate[0], w_up[0], w_down[0])
    return pl.pallas_call(
        finish,
        out_shape=(
            jax.ShapeDtypeStruct((1, 3, 16 * DW), BF),
            jax.ShapeDtypeStruct((1, 3, 16 * DW), BF),
            jax.ShapeDtypeStruct((1, DW, 2 * H), BF),
            jax.ShapeDtypeStruct((1, DW, 2 * H), BF),
            jax.ShapeDtypeStruct((1, 2 * H, DW), BF),
        ),
        in_specs=[vmem, hbm, hbm, hbm],
        out_specs=(hbm,) * 5,
        scratch_shapes=[V((2, 1, 3, 16 * DW), BF), D((3, 4)), D((2,))],
        compiler_params=pltpu.CompilerParams(vmem_limit_bytes=16 * 2**20),
        name="finish",
    )(seen, gg, gu, gd)


def solution(mesh):
    in_specs = (
        P("section", "col", "row"),
        P("section", "col", "row"),
        P("section", "col", "row"),
        P("section", "row", "col"),
        P("section", "row", "col"),
        P("section", "col", "row"),
    )
    out_specs = (
        P("section", ("row", "col"), None),
        P("section", ("row", "col"), None),
        P("section", "row", "col"),
        P("section", "row", "col"),
        P("section", "col", "row"),
    )
    return jax.shard_map(body, mesh=mesh, in_specs=in_specs, out_specs=out_specs, check_vma=False)
```
